32 devices in a mesh: dp: 8 (over z, x), tensor: 4 (over y, core).
Axes of the slice: x: 2, y: 2, z: 4, core: 2. Of those that a mesh axis runs over, the one named last changes fastest.
Arguments:
- hidden_in: bfloat16 [8192, 768], P(('dp', 'tensor')), may hold values from -6 to 6
- segment_ids: int32 [8, 1024], P('dp'), may hold values from 0 to 3, never falling along the last dimension, each value on 1 to 512 neighbouring positions
- expert_route: int32 [8192], P(('dp', 'tensor')), may hold values from 0 to 7, as said below
- slot_index: int32 [8192], P(('dp', 'tensor')), may hold values from 0 to 47, as said below
- norm1_gain: float32 [768], replicated, may hold values from 0.1 to 1.9
- w_query: bfloat16 [768, 768], P(None, 'tensor'), may hold values from -0.21875 to 0.21875
- w_key: bfloat16 [768, 768], P(None, 'tensor'), may hold values from -0.21875 to 0.21875
- w_value: bfloat16 [768, 768], P(None, 'tensor'), may hold values from -0.21875 to 0.21875
- w_out: bfloat16 [768, 768], P('tensor'), may hold values from -0.875 to 0.875
- rel_bias: float32 [32, 12], P(None, 'tensor'), may hold values from -4 to 4
- norm2_gain: float32 [768], replicated, may hold values from 0.1 to 1.9
- w_router: float32 [768, 8], replicated, may hold values from -0.109375 to 0.109375
- w_up: bfloat16 [8, 768, 3072], P('dp', None, 'tensor'), may hold values from -0.4375 to 0.4375
- w_down: bfloat16 [8, 3072, 768], P('dp', 'tensor'), may hold values from -0.875 to 0.875
- out_grad: bfloat16 [8192, 768], P(('dp', 'tensor')), may hold values from -6 to 6
Outputs:
- layer_out: bfloat16 [8192, 768], P(('dp', 'tensor'))
- input_grad: float32 [8192, 768], P(('dp', 'tensor'))
- norm1_gain_grad: float32 [768], replicated
- w_query_grad: float32 [768, 768], P(None, 'tensor')
- w_key_grad: float32 [768, 768], P(None, 'tensor')
- w_value_grad: float32 [768, 768], P(None, 'tensor')
- w_out_grad: float32 [768, 768], P('tensor')
- rel_bias_grad: float32 [32, 12], P(None, 'tensor')
- norm2_gain_grad: float32 [768], replicated
- w_router_grad: float32 [768, 8], replicated
- w_up_grad: float32 [8, 768, 3072], P('dp', None, 'tensor')
- w_down_grad: float32 [8, 3072, 768], P('dp', 'tensor')
The draws below stay inside these ranges and needn't reach their ends.
Inputs may be any that keep to these rules, and one draw needn't show every extreme that they name: `expert_route`: in each aligned block of 256 tokens each expert is named at most 48 times; in every block one expert, the same for all blocks, is named exactly 48 times; every expert is named somewhere. `slot_index`: tokens of one aligned block of 256 that name the same expert have different slots.
All inputs are finite; a program needn't handle non-finite values.
Results may differ from the reference program's by a relative error of at most 0.022.
Values may be sent and summed in bfloat16 or wider, within the bound.
No kernel may reach another device: no remote copies, remote signals or barrier semaphores. Data moves between devices by JAX's collectives and lax.ppermute only.
A program may use at most 192 MiB of HBM per device.

```python
import math
import jax
import jax.numpy as jnp
import numpy as np
from jax import lax

D = 768
HEADS = 12
FF = 3072
BUCKETS = 32
SEQ_LEN = 1024
ROWS = 256
SEQS = 8
TOKENS = 8192
EXPERTS = 8
C_SEND = 48
CAPACITY = 1536
N_DP = 8
N_TENSOR = 4


def assign_slots(key):
    send_total = EXPERTS * C_SEND
    forced = jax.random.randint(jax.random.fold_in(key, 11), (), 0, EXPERTS)
    ids_all = jnp.arange(send_total, dtype=jnp.int32)

    def one_block(block_key):
        score_key, order_key = jax.random.split(block_key)
        scores = jax.random.permutation(score_key, send_total).astype(jnp.int32)
        scores = jnp.where(ids_all // C_SEND == forced, scores - send_total, scores)
        picked = jnp.argsort(scores, stable=True)[:ROWS].astype(jnp.int32)
        return picked[jax.random.permutation(order_key, ROWS)]
    block_keys = jax.random.split(jax.random.fold_in(key, 12), N_DP * N_TENSOR)
    chosen = jax.vmap(one_block)(block_keys).reshape(-1).astype(jnp.int32)
    return (chosen // C_SEND, chosen % C_SEND)


def draw_expert_route(key, part):
    routes, slots = assign_slots(key)
    return routes


def draw_slot_index(key, part):
    routes, slots = assign_slots(key)
    return slots


def block_scale(rng, dims, cuts, smallest, high):
    def one(dim, blocks):
        steps = jax.random.uniform(jax.random.fold_in(jax.random.fold_in(rng, 6), dim), (blocks,), jnp.float32, smallest / len(cuts), high / len(cuts))
        return jnp.repeat(jnp.exp(steps), dims[dim] // blocks).reshape((-1,) + (1,) * (len(dims) - dim - 1))

    level = one(*cuts[0])
    for cut in cuts[1:]:
        level = level * one(*cut)
    return level


def profile(amount, total, bound, lean):
    weights = [(1 << 20) // math.isqrt(rank ** lean) + 1 for rank in range(2, amount + 1)]
    surplus, holding = total - bound - (amount - 1), [1] * (amount - 1)
    while surplus > 0:
        free = [i for i in range(amount - 1) if holding[i] < bound]
        pool, left = sum([weights[i] for i in free]), surplus
        for i in free:
            extra = min(bound - holding[i], max(1, left * weights[i] // pool), surplus)
            holding[i] = holding[i] + extra
            surplus = surplus - extra
    return np.array([bound] + holding)


def uneven_parts(rng, count, total, limit, skew):
    if count == 2:
        one = jax.random.randint(rng, (), max(1, total - limit), min(limit, total - 1) + 1)
        return jnp.stack([one, total - one])
    lengths = jnp.asarray(profile(count, total, limit, skew), jnp.int32)
    couples = (count - 1) // 2
    source_of, sink = lengths[1:1 + 2 * couples:2], lengths[2:2 + 2 * couples:2]
    slack = jnp.minimum(source_of - 1, limit - sink)
    moved = jax.random.randint(jax.random.fold_in(rng, 1), (couples,), 0, 1 << 20) % (slack + 1)
    lengths = lengths.at[1:1 + 2 * couples:2].set(source_of - moved).at[2:2 + 2 * couples:2].set(sink + moved)
    return lengths[jax.random.permutation(jax.random.fold_in(rng, 2), count)]


def bell_draw(key, dims, deviation, most, cuts=(), kind=jnp.bfloat16):
    values = jax.random.normal(key, dims, jnp.float32) * deviation
    if len(cuts) > 0:
        values = block_scale(key, dims, cuts, -0.22, 0.18) * values
    return jnp.clip(values, min=-most, max=most).astype(kind)


def setup_inputs(seed: int = 0) -> dict:
    seeds = jax.random.split(jax.random.key(seed), 16)
    hidden_in = bell_draw(seeds[0], (TOKENS, D), 1.0, 6.0, ((0, 32),))
    segment_ids = jax.vmap(lambda own: jnp.searchsorted(jnp.cumsum(uneven_parts(own, 4, SEQ_LEN, SEQ_LEN // 2, 1)), jnp.arange(SEQ_LEN), side="right"))(jax.random.split(seeds[1], SEQS)).reshape((SEQS, SEQ_LEN)).astype(jnp.int32)
    expert_route = draw_expert_route(jax.random.fold_in(seeds[15], 71), 0)
    slot_index = draw_slot_index(jax.random.fold_in(seeds[15], 71), 0)
    norm1_gain = jnp.clip(1.0 + 0.18 * jax.random.normal(seeds[4], (D,), jnp.float32), 0.1, 1.9)
    w_query = bell_draw(seeds[5], (D, D), D ** -0.5, 0.21875, ((1, 4),))
    w_key = bell_draw(seeds[6], (D, D), D ** -0.5, 0.21875, ((1, 4),))
    w_value = bell_draw(seeds[7], (D, D), D ** -0.5, 0.21875, ((1, 4),))
    w_out = bell_draw(seeds[8], (D, D), (D // 16) ** -0.5, 0.875, ((0, 4),))
    rel_bias = bell_draw(seeds[9], (BUCKETS, HEADS), 1.0, 4.0, ((1, 4),), jnp.float32)
    norm2_gain = jnp.clip(1.0 + 0.18 * jax.random.normal(seeds[10], (D,), jnp.float32), 0.1, 1.9)
    w_router = bell_draw(seeds[11], (D, EXPERTS), (4 * D) ** -0.5, 0.109375, (), jnp.float32)
    w_up = bell_draw(seeds[12], (EXPERTS, D, FF), (D // 4) ** -0.5, 0.4375, ((0, 8), (2, 4)))
    w_down = bell_draw(seeds[13], (EXPERTS, FF, D), (FF // (EXPERTS * EXPERTS) + 1) ** -0.5, 0.875, ((0, 8), (1, 4)))
    out_grad = bell_draw(seeds[14], (TOKENS, D), 1.0, 6.0, ((0, 32),))
    return dict(hidden_in=hidden_in, segment_ids=segment_ids, expert_route=expert_route, slot_index=slot_index, norm1_gain=norm1_gain, w_query=w_query, w_key=w_key, w_value=w_value, w_out=w_out, rel_bias=rel_bias, norm2_gain=norm2_gain, w_router=w_router, w_up=w_up, w_down=w_down, out_grad=out_grad)


highest = lax.Precision.HIGHEST
epsilon = 1e-06
masked_score = -1000000000.0

@jax.custom_vjp
def low(v):
    return lax.optimization_barrier(v.astype(jnp.bfloat16)).astype(jnp.float32)

@jax.custom_vjp
def low_back(v):
    return v

def low_keep(v):
    return (low(v), None)

def low_pass(kept, grad):
    return (grad,)

def back_keep(v):
    return (v, None)

def back_low(kept, grad):
    return (low(grad),)
low.defvjp(low_keep, low_pass)
low_back.defvjp(back_keep, back_low)

def bucket_of(offsets, bucket_count):
    half_count = bucket_count // 2
    exact_count = half_count // 2
    upward = (offsets > 0).astype(np.int32) * half_count
    distance = np.abs(offsets)
    scaled = np.log(np.maximum(distance, 1) / exact_count) / np.log(128 / exact_count) * (half_count - exact_count)
    distant = np.minimum(exact_count + np.floor(scaled).astype(np.int32), half_count - 1)
    return (upward + np.where(distance < exact_count, distance, distant)).astype(np.int32)

def rms_norm(values, gain_vec):
    scale_row = lax.rsqrt(lax.optimization_barrier(jnp.mean(values * values, axis=-1, keepdims=True)) + epsilon)
    return values * scale_row * gain_vec

def forward_pass(floats, segment_ids, expert_route, slot_index):
    hidden_in, norm1_gain, w_query, w_key, w_value, w_out, rel_bias, norm2_gain, w_router, w_up, w_down = floats
    token_count, model_width = hidden_in.shape
    seq_count, seq_len = segment_ids.shape
    head_count = rel_bias.shape[1]
    head_size = model_width // head_count
    score_scale = head_size ** (-0.5)
    normed = low_back(low(rms_norm(hidden_in, norm1_gain)))
    shape_seq = (seq_count, seq_len, head_count, head_size)
    queries = low_back(low(jnp.dot(normed, w_query, precision=highest))).reshape(shape_seq)
    keys_all = low_back(low(jnp.dot(normed, w_key, precision=highest))).reshape(shape_seq)
    values_all = low_back(low(jnp.dot(normed, w_value, precision=highest))).reshape(shape_seq)
    offsets = np.arange(seq_len)[None, :] - np.arange(seq_len)[:, None]
    bucket_grid = jnp.asarray(bucket_of(offsets, rel_bias.shape[0]))
    bias_grid = jnp.transpose(rel_bias[bucket_grid], (2, 0, 1))

    def one_sequence(carry_in, inputs):
        query_seq, key_seq, value_seq, segment_row = inputs
        scores = jnp.einsum('qhd,khd->hqk', query_seq, key_seq, precision=highest) * score_scale + bias_grid
        scores = low_back(scores)
        same_doc = segment_row[:, None] == segment_row[None, :]
        masked = jnp.where(same_doc[None], scores, masked_score)
        prob_low = low(jax.nn.softmax(masked, axis=-1))
        return (carry_in, jnp.einsum('hqk,khd->qhd', prob_low, value_seq, precision=highest))
    unused, attended = lax.scan(jax.checkpoint(one_sequence), jnp.zeros((), jnp.float32), (queries, keys_all, values_all, segment_ids))
    attended = low_back(low(attended.reshape(token_count, model_width)))
    middle = hidden_in + low_back(jnp.dot(attended, w_out, precision=highest))
    normed_two = low_back(low(rms_norm(middle, norm2_gain)))
    router_probs = jax.nn.softmax(jnp.dot(normed_two, w_router, precision=highest), axis=-1)
    expert_count = w_router.shape[1]
    chosen = (expert_route[:, None] == jnp.arange(expert_count, dtype=jnp.int32)[None, :]).astype(jnp.float32)
    gate_value = lax.optimization_barrier(jnp.sum(router_probs * chosen, axis=-1))
    source = jnp.arange(token_count, dtype=jnp.int32) // ROWS
    position = expert_route * CAPACITY + source * C_SEND + slot_index
    buffer = jnp.zeros((expert_count * CAPACITY, model_width), jnp.float32).at[position].set(normed_two)
    buffer = low_back(buffer)

    def one_expert(inputs):
        expert_rows, up_matrix, down_matrix = inputs
        pre_act = low_back(jnp.dot(expert_rows, up_matrix, precision=highest))
        active = low_back(low(jax.nn.gelu(pre_act, approximate=True)))
        return low_back(low(jnp.dot(active, down_matrix, precision=highest)))
    produced = lax.map(jax.checkpoint(one_expert), (buffer.reshape(expert_count, CAPACITY, model_width), w_up, w_down))
    returned = produced.reshape(expert_count * CAPACITY, model_width)[position]
    return middle + gate_value[:, None] * returned

def reference(hidden_in, segment_ids, expert_route, slot_index, norm1_gain, w_query, w_key, w_value, w_out, rel_bias, norm2_gain, w_router, w_up, w_down, out_grad):
    floats = tuple((array.astype(jnp.float32) for array in (hidden_in, norm1_gain, w_query, w_key, w_value, w_out, rel_bias, norm2_gain, w_router, w_up, w_down)))

    def closed(*weights):
        return forward_pass(weights, segment_ids, expert_route, slot_index)
    output, pullback = jax.vjp(closed, *floats)
    gradients = pullback(out_grad.astype(jnp.float32))
    return (output.astype(jnp.bfloat16), gradients[0], gradients[1], gradients[2], gradients[3], gradients[4], gradients[5], gradients[6], gradients[7], gradients[8], gradients[9], gradients[10])
```

```python
import functools

import jax
import jax.numpy as jnp
import numpy as np
from jax import lax
from jax.experimental import pallas as pl
from jax.experimental.pallas import tpu as pltpu
from jax.sharding import PartitionSpec as P

highest = lax.Precision.HIGHEST
epsilon = 1e-06
apart = 2.0**30
near_reach = 128
vmem_bytes = 48 * 1024 * 1024


def bucket_of(offsets, bucket_count):
    half_count = bucket_count // 2
    exact_count = half_count // 2
    upward = (offsets > 0).astype(np.int32) * half_count
    distance = np.abs(offsets)
    scaled = (
        np.log(np.maximum(distance, 1) / exact_count)
        / np.log(128 / exact_count)
        * (half_count - exact_count)
    )
    distant = np.minimum(exact_count + np.floor(scaled).astype(np.int32), half_count - 1)
    return (upward + np.where(distance < exact_count, distance, distant)).astype(np.int32)


def rounded(values):
    return lax.optimization_barrier(values.astype(jnp.bfloat16)).astype(jnp.float32)


def rms_forward(values, gain_vec):
    scale_row = lax.rsqrt(jnp.mean(values * values, axis=-1, keepdims=True) + epsilon)
    return (values * scale_row * gain_vec, scale_row)


def rms_backward(values, scale_row, gain_vec, normed_grad):
    gain_grad = jnp.sum(normed_grad * values * scale_row, axis=0)
    grad_hat = normed_grad * gain_vec
    row_inner = jnp.mean(grad_hat * values, axis=-1, keepdims=True)
    return (scale_row * (grad_hat - values * scale_row * scale_row * row_inner), gain_grad)


def swap(values, axis_name, bits):
    count = lax.axis_size(axis_name)
    return lax.ppermute(values, axis_name, [(i, i ^ bits) for i in range(count)])


def power_of_two(axis_name):
    count = lax.axis_size(axis_name)
    return count <= 8 and count & (count - 1) == 0


def exchange(chunks):
    return lax.all_to_all(chunks, "dp", split_axis=0, concat_axis=0, tiled=True)


def exchange_four(chunks):
    parts = [swap(chunks[k], "tensor", k) for k in range(1, chunks.shape[0])]
    return [chunks[0]] + parts


def gather_four(values):
    across = swap(values, "tensor", 2)
    beside = swap(values, "tensor", 1)
    return [values, beside, across, swap(across, "tensor", 1)]


def tie(*arrays):
    return lax.optimization_barrier(arrays)


def pick(stacked, index):
    return lax.dynamic_index_in_dim(stacked, index, axis=0, keepdims=False)


def sum_dp(values):
    count = lax.axis_size("dp")
    rows, width = values.shape
    parts = exchange(values.astype(jnp.bfloat16).reshape(count, rows // count, width))
    total = jnp.sum(parts.astype(jnp.float32), axis=0, keepdims=True).astype(jnp.bfloat16)
    return exchange(jnp.broadcast_to(total, parts.shape)).reshape(rows, width).astype(jnp.float32)


def sum_all(values):
    if not (power_of_two("dp") and power_of_two("tensor")):
        return lax.psum(values, ("dp", "tensor"))
    for axis_name in ("tensor", "dp"):
        bits = 1
        while bits < lax.axis_size(axis_name):
            values = values + swap(values, axis_name, bits)
            bits *= 2
    return values


def smooth(values):
    return jax.nn.gelu(values, approximate=True)


def gelu_back(pre_act, active_grad):
    output_unused, pullback = jax.vjp(smooth, pre_act)
    (pre_grad,) = pullback(active_grad.astype(jnp.float32))
    return pre_grad.astype(jnp.bfloat16)


def dot_nt(left, right):
    return lax.dot_general(
        left, right, (((1,), (1,)), ((), ())), preferred_element_type=jnp.float32
    )


def dot_nn(left, right):
    return lax.dot_general(
        left, right, (((1,), (0,)), ((), ())), preferred_element_type=jnp.float32
    )


def fill_slab(line_ref, slab_ref, heads, block):
    slab_rows = slab_ref.shape[1]
    near_rows = block + 2 * near_reach
    near_start = (slab_rows - near_rows + block) // 2 - block // 2
    line_len = line_ref.shape[1]
    for h in range(heads):
        line = line_ref[h : h + 1, :]
        rolled = pltpu.roll(
            jnp.broadcast_to(line, (block, line_len)), 0, axis=1, stride=1, stride_axis=0
        )
        slab_ref[h, near_start : near_start + near_rows, :] = rolled[:, block:].T
        slab_ref[h, :near_start, :] = jnp.broadcast_to(line[:, :1], (near_start, block))
        after = near_start + near_rows
        slab_ref[h, after:, :] = jnp.broadcast_to(
            line[:, line_len - 1 :], (slab_rows - after, block)
        )


def forward_kernel(
    heads,
    block,
    me_ref,
    normed_ref,
    wq_ref,
    wk_ref,
    wv_ref,
    line_ref,
    segment_ref,
    attended_ref,
    q_ref,
    k_ref,
    v_ref,
    total_ref,
    attended_t_ref,
    slab_ref,
    vt_ref,
):
    me = me_ref[0]
    groups, rows, width = normed_ref.shape
    local_width = v_ref.shape[1]
    wide = q_ref.shape[1]
    head_size = local_width // heads
    seq_len = groups * rows
    fill_slab(line_ref, slab_ref, heads, block)
    lane = lax.broadcasted_iota(jnp.int32, (rows, wide), 1)
    for j in range(groups):
        part = normed_ref[j ^ me]
        here = slice(j * rows, (j + 1) * rows)
        mark = lane - local_width == segment_ref[here, :]
        queries = dot_nn(part, wq_ref[...]).astype(jnp.bfloat16).astype(jnp.float32)
        queries = queries * head_size ** (-0.5)
        q_ref[here, :] = jnp.where(mark, -apart, queries).astype(jnp.bfloat16)
        keys = dot_nn(part, wk_ref[...])
        other = jnp.logical_and(lane >= local_width, jnp.logical_not(mark))
        k_ref[here, :] = jnp.where(other, 1.0, keys).astype(jnp.bfloat16)
        values = dot_nn(part, wv_ref[...])
        v_ref[here, :] = values.astype(jnp.bfloat16)
        vt_ref[:, here] = values.T.astype(jnp.bfloat16)
    blocks = seq_len // block
    block_lane = lax.broadcasted_iota(jnp.int32, (block, wide), 1)

    def one_block(i, carry):
        start = pl.multiple_of(i * block, block)
        offset = pl.multiple_of((blocks - 1 - i) * block, block)
        query_blk = q_ref[pl.ds(start, block), :]
        outputs = []
        for h in range(heads):
            mine = jnp.logical_or(
                jnp.logical_and(block_lane >= h * head_size, block_lane < (h + 1) * head_size),
                block_lane >= local_width,
            )
            query = jnp.where(mine, query_blk, jnp.zeros_like(query_blk))
            scores = dot_nt(k_ref[...], query) + slab_ref[h, pl.ds(offset, seq_len), :]
            peak = jnp.max(scores, axis=0, keepdims=True)
            weights = jnp.exp(scores - peak)
            total = jnp.sum(weights, axis=0, keepdims=True)
            out = dot_nn(
                vt_ref[h * head_size : (h + 1) * head_size, :], weights.astype(jnp.bfloat16)
            )
            outputs.append(out * (1.0 / total))
            total_ref[h : h + 1, pl.ds(start, block)] = peak + jnp.log(total)
        outputs = jnp.concatenate(outputs, axis=0)
        attended_t_ref[:, pl.ds(start, block)] = outputs
        attended_ref[i ^ me] = outputs.T.astype(jnp.bfloat16)
        return carry

    lax.fori_loop(0, blocks, one_block, 0)


def backward_kernel(
    heads,
    block,
    me_ref,
    q_ref,
    k_ref,
    v_ref,
    total_ref,
    line_ref,
    attended_t_ref,
    grad_ref,
    dqkv_ref,
    near_ref,
    far_ref,
    slab_ref,
    diag_ref,
    kt_ref,
    qt_ref,
    out_ref,
    out_t_ref,
    inner_ref,
    p_ref,
    ds_ref,
    grad_t_ref,
):
    me = me_ref[0]
    seq_len, local_width = v_ref.shape
    wide = q_ref.shape[1]
    head_size = local_width // heads
    blocks = seq_len // block
    fill_slab(line_ref, slab_ref, heads, block)
    diag_ref[...] = jnp.zeros_like(diag_ref)
    for j in range(blocks):
        here = slice(j * block, (j + 1) * block)
        grads = grad_ref[j ^ me]
        out_ref[here, :] = grads
        grads_t = grads.astype(jnp.float32).T
        out_t_ref[:, here] = grads_t.astype(jnp.bfloat16)
        products = grads_t * attended_t_ref[:, here]
        for h in range(heads):
            inner_ref[h : h + 1, here] = jnp.sum(
                products[h * head_size : (h + 1) * head_size], axis=0, keepdims=True
            )
        kt_ref[:, here] = k_ref[here, :].astype(jnp.float32).T.astype(jnp.bfloat16)
        qt_ref[:, here] = q_ref[here, :].astype(jnp.float32).T.astype(jnp.bfloat16)
    wide_lane = lax.broadcasted_iota(jnp.int32, (block, wide), 1)
    lane = lax.broadcasted_iota(jnp.int32, (block, local_width), 1)
    for h in range(heads):
        low, high = h * head_size, (h + 1) * head_size
        mine = jnp.logical_or(
            jnp.logical_and(wide_lane >= low, wide_lane < high), wide_lane >= local_width
        )
        head_lanes = jnp.logical_and(lane >= low, lane < high)

        def one_block(i, carry):
            start = pl.multiple_of(i * block, block)
            offset = pl.multiple_of((blocks - 1 - i) * block, block)
            query_blk = q_ref[pl.ds(start, block), :]
            query = jnp.where(mine, query_blk, jnp.zeros_like(query_blk))
            grad_blk = out_ref[pl.ds(start, block), :]
            grad = jnp.where(head_lanes, grad_blk, jnp.zeros_like(grad_blk))
            scores = dot_nt(k_ref[...], query) + slab_ref[h, pl.ds(offset, seq_len), :]
            probs = jnp.exp(scores - total_ref[h : h + 1, pl.ds(start, block)])
            prob_grad = dot_nt(v_ref[...], grad)
            score_grad = probs * (prob_grad - inner_ref[h : h + 1, pl.ds(start, block)])
            score_low = score_grad.astype(jnp.bfloat16)
            p_ref[:, pl.ds(start, block)] = probs.astype(jnp.bfloat16)
            ds_ref[:, pl.ds(start, block)] = score_low
            diag_ref[h, pl.ds(offset, seq_len), :] += score_grad
            grad_t_ref[low:high, pl.ds(start, block)] = dot_nn(
                kt_ref[low:high, :], score_low
            ) * head_size ** (-0.5)
            return carry

        lax.fori_loop(0, blocks, one_block, 0)
        grad_t_ref[local_width + low : local_width + high, :] = dot_nt(
            qt_ref[low:high, :], ds_ref[...]
        )
        grad_t_ref[2 * local_width + low : 2 * local_width + high, :] = dot_nt(
            out_t_ref[low:high, :], p_ref[...]
        )
    for j in range(blocks):
        here = slice(j * block, (j + 1) * block)
        dqkv_ref[j ^ me] = grad_t_ref[:, here].T.astype(jnp.bfloat16)
    slab_rows = diag_ref.shape[1]
    near_rows = block + 2 * near_reach
    near_start = (slab_rows - near_rows) // 2
    line_len = line_ref.shape[1]
    row_id = lax.broadcasted_iota(jnp.int32, (block, line_len), 0)
    for h in range(heads):
        near = diag_ref[h, near_start : near_start + near_rows, :].T
        near = jnp.concatenate([jnp.zeros((block, line_len - near_rows), jnp.float32), near], axis=1)
        bit = 1
        while bit < block:
            near = jnp.where(
                (row_id // bit) % 2 == 1, pltpu.roll(near, line_len - bit, axis=1), near
            )
            bit *= 2
        near_ref[h : h + 1, :] = jnp.sum(near, axis=0, keepdims=True)
        far_ref[h : h + 1, :] = jnp.sum(diag_ref[h, :near_start, :], axis=0, keepdims=True)
        far_ref[heads + h : heads + h + 1, :] = jnp.sum(
            diag_ref[h, near_start + near_rows :, :], axis=0, keepdims=True
        )


def in_vmem(count):
    return [pl.BlockSpec(memory_space=pltpu.VMEM)] * count


def attention_forward(me, normed, w_query, w_key, w_value, line, segment_col):
    groups, rows, width = normed.shape
    local_width = w_query.shape[1]
    heads = line.shape[0]
    wide = -(-(local_width + 4) // 128) * 128
    pad = ((0, 0), (0, wide - local_width))
    seq_len = groups * rows
    return pl.pallas_call(
        functools.partial(forward_kernel, heads, rows),
        out_shape=(
            jax.ShapeDtypeStruct((groups, rows, local_width), jnp.bfloat16),
            jax.ShapeDtypeStruct((seq_len, wide), jnp.bfloat16),
            jax.ShapeDtypeStruct((seq_len, wide), jnp.bfloat16),
            jax.ShapeDtypeStruct((seq_len, local_width), jnp.bfloat16),
            jax.ShapeDtypeStruct((heads, seq_len), jnp.float32),
            jax.ShapeDtypeStruct((local_width, seq_len), jnp.float32),
        ),
        in_specs=[pl.BlockSpec(memory_space=pltpu.SMEM)] + in_vmem(6),
        out_specs=tuple(in_vmem(6)),
        scratch_shapes=[
            pltpu.VMEM((heads, 2 * seq_len - rows, rows), jnp.float32),
            pltpu.VMEM((local_width, seq_len), jnp.bfloat16),
        ],
        compiler_params=pltpu.CompilerParams(vmem_limit_bytes=vmem_bytes),
        cost_estimate=pl.CostEstimate(
            flops=seq_len * width * local_width * 6 + seq_len * seq_len * wide * heads * 4,
            bytes_accessed=6 * 1024 * 1024,
            transcendentals=seq_len * seq_len * heads,
        ),
        name="attention_forward",
    )(me, normed, jnp.pad(w_query, pad), jnp.pad(w_key, pad), w_value, line, segment_col)


def attention_backward(
    me, queries, keys_all, values_all, totals, line, attended_t, out_grads
):
    groups, rows, local_width = out_grads.shape
    seq_len, wide = queries.shape
    heads, line_len = line.shape
    return pl.pallas_call(
        functools.partial(backward_kernel, heads, rows),
        out_shape=(
            jax.ShapeDtypeStruct((groups, rows, 3 * local_width), jnp.bfloat16),
            jax.ShapeDtypeStruct((heads, line_len), jnp.float32),
            jax.ShapeDtypeStruct((2 * heads, rows), jnp.float32),
        ),
        in_specs=[pl.BlockSpec(memory_space=pltpu.SMEM)] + in_vmem(7),
        out_specs=tuple(in_vmem(3)),
        scratch_shapes=[
            pltpu.VMEM((heads, 2 * seq_len - rows, rows), jnp.float32),
            pltpu.VMEM((heads, 2 * seq_len - rows, rows), jnp.float32),
            pltpu.VMEM((wide, seq_len), jnp.bfloat16),
            pltpu.VMEM((wide, seq_len), jnp.bfloat16),
            pltpu.VMEM((seq_len, local_width), jnp.bfloat16),
            pltpu.VMEM((local_width, seq_len), jnp.bfloat16),
            pltpu.VMEM((heads, seq_len), jnp.float32),
            pltpu.VMEM((seq_len, seq_len), jnp.bfloat16),
            pltpu.VMEM((seq_len, seq_len), jnp.bfloat16),
            pltpu.VMEM((3 * local_width, seq_len), jnp.float32),
        ],
        compiler_params=pltpu.CompilerParams(vmem_limit_bytes=vmem_bytes),
        cost_estimate=pl.CostEstimate(
            flops=seq_len * seq_len * wide * heads * 10,
            bytes_accessed=6 * 1024 * 1024,
            transcendentals=seq_len * seq_len * heads,
        ),
        name="attention_backward",
    )(me, queries, keys_all, values_all, totals, line, attended_t, out_grads)


def per_device(
    hidden_in,
    segment_ids,
    expert_route,
    slot_index,
    norm1_gain,
    w_query,
    w_key,
    w_value,
    w_out,
    rel_bias,
    norm2_gain,
    w_router,
    w_up,
    w_down,
    out_grad,
):
    row_count, model_width = hidden_in.shape
    experts = w_router.shape[1]
    c_send = 3 * row_count // (2 * experts)
    slots = experts * c_send
    tensor_me = lax.axis_index("tensor").astype(jnp.int32)
    dp_me = lax.axis_index("dp").astype(jnp.int32)
    me = tensor_me.reshape(1)
    heads_here = rel_bias.shape[1]
    bucket_count = rel_bias.shape[0]
    local_width = w_query.shape[1]

    position = expert_route * c_send + slot_index

    def place(rows):
        return (
            jnp.zeros((slots, model_width), jnp.bfloat16)
            .at[position]
            .set(rows)
            .reshape(experts, c_send, model_width)
        )

    inputs_f = hidden_in.astype(jnp.float32)
    normed, scale_one = rms_forward(inputs_f, norm1_gain)
    normed_four = jnp.stack(gather_four(normed.astype(jnp.bfloat16)))

    grads_here = exchange(place(out_grad)).reshape(slots, model_width)
    grad_rows = jnp.concatenate([grads_here, swap(grads_here, "tensor", 1)])

    up_local, down_local = w_up[0], w_down[0]
    early = down_local.shape[0] // 4
    normed_four, w_out_here, down_first = tie(normed_four, w_out, down_local[:early])
    w_out_four = jnp.concatenate(gather_four(w_out_here), axis=0)
    down_early = swap(down_first, "tensor", 2)

    line_len = 2 * row_count + 2 * near_reach
    line_offsets = np.arange(line_len) - (row_count + near_reach)
    line_buckets = bucket_of(line_offsets, bucket_count)
    lookup = jnp.asarray(
        (line_buckets[:, None] == np.arange(bucket_count)[None, :]).astype(np.float32)
    )
    line = jnp.einsum("rb,bh->hr", lookup, rel_bias, precision=highest)
    segment_col = segment_ids.reshape(-1, 1)
    attended_four, queries, keys_all, values_all, totals, attended_t = attention_forward(
        me, normed_four, w_query, w_key, w_value, line, segment_col
    )
    attended_four, down_early, w_out_four, grad_rows = tie(
        attended_four, down_early, w_out_four, grad_rows
    )
    attended_here = jnp.concatenate(exchange_four(attended_four), axis=1)
    attended_here, up_sent, down_rest = tie(attended_here, up_local, down_local[early:])
    up_far = swap(up_sent, "tensor", 2)
    down_late = swap(down_rest, "tensor", 2)
    middle = inputs_f + jnp.dot(attended_here, w_out_four, preferred_element_type=jnp.float32)
    normed_two, scale_two = rms_forward(middle, norm2_gain)
    normed_two_low = normed_two.astype(jnp.bfloat16)

    rows_here = exchange(place(normed_two_low)).reshape(slots, model_width)
    rows_here, up_far = tie(rows_here, up_far)
    expert_rows = jnp.concatenate([rows_here, swap(rows_here, "tensor", 1)])

    router_logits = jnp.dot(expert_rows.astype(jnp.float32), w_router, precision=highest)
    router_probs = jax.nn.softmax(router_logits, axis=-1)
    chosen_row = (jnp.arange(experts, dtype=jnp.int32) == dp_me).astype(jnp.float32)
    row_gate = jnp.sum(router_probs * chosen_row, axis=-1, keepdims=True)
    produced_grad = (row_gate * grad_rows.astype(jnp.float32)).astype(jnp.bfloat16)

    def back(weights):
        return jnp.einsum(
            "cd,fd->cf", produced_grad, weights, preferred_element_type=jnp.float32
        ).astype(jnp.bfloat16)

    def to_rows(grads, weights):
        return jnp.einsum("cf,df->cd", grads, weights, preferred_element_type=jnp.float32)

    pre_near = jnp.dot(expert_rows, up_local, preferred_element_type=jnp.float32)
    active_near = smooth(pre_near).astype(jnp.bfloat16)
    produced_near = jnp.dot(active_near, down_local, preferred_element_type=jnp.float32)
    pre_grad_near = gelu_back(pre_near, back(down_local))
    rows_near = to_rows(pre_grad_near, up_local)
    rows_near, down_late = tie(rows_near, down_late)
    down_far = jnp.concatenate([down_early, down_late])
    pre_far = jnp.dot(expert_rows, up_far, preferred_element_type=jnp.float32)
    active_far = smooth(pre_far).astype(jnp.bfloat16)
    produced_part = produced_near + jnp.dot(
        active_far, down_far, preferred_element_type=jnp.float32
    )
    produced_came = swap(produced_part[slots:].astype(jnp.bfloat16), "tensor", 1)
    produced = (produced_part[:slots] + produced_came.astype(jnp.float32)).astype(jnp.bfloat16)
    pre_grad_far = gelu_back(pre_far, back(down_far))
    row_part = rows_near + to_rows(pre_grad_far, up_far)
    row_came = swap(row_part[slots:].astype(jnp.bfloat16), "tensor", 1)
    buffer_grad = rounded(row_part[:slots] + row_came.astype(jnp.float32))
    gate_grad = jnp.sum(
        grads_here.astype(jnp.float32) * produced.astype(jnp.float32), axis=-1, keepdims=True
    )
    logit_grad = router_probs[:slots] * (chosen_row - row_gate[:slots]) * gate_grad
    router_grad = jnp.einsum(
        "td,te->de", rows_here.astype(jnp.float32), logit_grad, precision=highest
    )
    rows_back = (
        buffer_grad + jnp.einsum("te,de->td", logit_grad, w_router, precision=highest)
    ).astype(jnp.bfloat16)

    grads_back = exchange(rows_back.reshape(experts, c_send, model_width))
    grads_back, produced = tie(grads_back, produced)
    normed_two_grad = grads_back.reshape(slots, model_width)[position].astype(jnp.float32)
    grad_out = out_grad.astype(jnp.float32)
    middle_part, gain_two_grad = rms_backward(middle, scale_two, norm2_gain, normed_two_grad)
    middle_grad = grad_out + middle_part
    middle_grad_low = middle_grad.astype(jnp.bfloat16)
    attended_grad = jnp.einsum(
        "td,wd->tw", middle_grad_low, w_out_four, preferred_element_type=jnp.float32
    ).astype(jnp.bfloat16)
    grad_four = jnp.stack(
        exchange_four(
            jnp.stack(jnp.split(attended_grad, w_out_four.shape[0] // local_width, axis=1))
        )
    )

    def of_weights(left, right):
        return jnp.einsum("cd,cf->df", left, right, preferred_element_type=jnp.float32)

    down_sent = of_weights(active_far, produced_grad).astype(jnp.bfloat16)
    down_sent, grad_four, middle_sent = tie(down_sent, grad_four, middle_grad_low)
    down_came = swap(down_sent, "tensor", 2)
    down_grad = of_weights(active_near, produced_grad) + down_came.astype(jnp.float32)
    up_sent = of_weights(expert_rows, pre_grad_far).astype(jnp.bfloat16)

    returned = exchange(produced.reshape(experts, c_send, model_width))
    middle_four = jnp.stack(gather_four(middle_sent))

    dqkv, near_grad, far_grad = attention_backward(
        me, queries, keys_all, values_all, totals, line, attended_t, grad_four
    )
    far_here = jnp.sum(far_grad, axis=1).reshape(2, heads_here)
    rel_grad = jnp.einsum("rb,hr->bh", lookup, near_grad, precision=highest)
    rel_grad = rel_grad.at[bucket_count // 2 - 1].add(far_here[0])
    rel_grad = rel_grad.at[bucket_count - 1].add(far_here[1])

    def of_tokens(left, right):
        return jnp.einsum("ktd,ktw->dw", left, right, preferred_element_type=jnp.float32)

    out_weight_grad = of_tokens(middle_four, attended_four).astype(jnp.bfloat16)
    qkv_weight_grad = of_tokens(normed_four, dqkv).astype(jnp.bfloat16)
    dense = jnp.concatenate([qkv_weight_grad, out_weight_grad], axis=1)
    dense, returned = tie(dense, returned)
    dense = sum_dp(dense)
    returned = returned.reshape(slots, model_width)[position].astype(jnp.float32)
    token_probs = jax.nn.softmax(
        jnp.dot(normed_two_low.astype(jnp.float32), w_router, precision=highest), axis=-1
    )
    chosen = (expert_route[:, None] == jnp.arange(experts, dtype=jnp.int32)[None, :]).astype(
        jnp.float32
    )
    gate_value = jnp.sum(token_probs * chosen, axis=-1, keepdims=True)
    layer_out = (middle + gate_value * returned).astype(jnp.bfloat16)


    weights_qkv = jnp.concatenate([w_query, w_key, w_value], axis=1)
    normed_part = jnp.einsum(
        "ktw,dw->ktd", dqkv, weights_qkv, preferred_element_type=jnp.float32
    )
    beside = swap(jnp.stack([normed_part[1], normed_part[3]]).astype(jnp.bfloat16), "tensor", 1)
    beside = beside.astype(jnp.float32)
    across = swap((normed_part[2] + beside[1]).astype(jnp.bfloat16), "tensor", 2)
    up_sent, across = tie(up_sent, across)
    up_came = swap(up_sent, "tensor", 2)
    up_grad = of_weights(expert_rows, pre_grad_near) + up_came.astype(jnp.float32)
    normed_grad = rounded(normed_part[0] + beside[0] + across.astype(jnp.float32))
    input_part, gain_one_grad = rms_backward(inputs_f, scale_one, norm1_gain, normed_grad)
    input_grad = middle_grad + input_part

    rel_place = (
        jnp.arange(lax.axis_size("tensor"), dtype=jnp.int32)[:, None] == tensor_me
    ).astype(jnp.float32)
    rel_wide = rel_place[:, :, None] * rel_grad.T[None]
    flat = jnp.concatenate(
        [
            gain_one_grad.reshape(-1),
            gain_two_grad.reshape(-1),
            router_grad.reshape(-1),
            rel_wide.reshape(-1),
        ]
    )
    flat = sum_all(flat)
    gain_one_grad = flat[:model_width]
    gain_two_grad = flat[model_width : 2 * model_width]
    split = 2 * model_width + model_width * experts
    router_grad = flat[2 * model_width : split].reshape(model_width, experts)
    rel_all = flat[split:].reshape(-1, heads_here, bucket_count)
    rel_grad = pick(rel_all, tensor_me).T
    return (
        layer_out,
        input_grad,
        gain_one_grad,
        dense[:, :local_width],
        dense[:, local_width : 2 * local_width],
        dense[:, 2 * local_width : 3 * local_width],
        dense[:, 3 * local_width :].T,
        rel_grad,
        gain_two_grad,
        router_grad,
        up_grad[None],
        down_grad[None],
    )


def solution(mesh):
    return jax.shard_map(
        per_device,
        mesh=mesh,
        in_specs=(
            P(("dp", "tensor"), None),
            P("dp", None),
            P(("dp", "tensor")),
            P(("dp", "tensor")),
            P(),
            P(None, "tensor"),
            P(None, "tensor"),
            P(None, "tensor"),
            P("tensor", None),
            P(None, "tensor"),
            P(),
            P(),
            P("dp", None, "tensor"),
            P("dp", "tensor", None),
            P(("dp", "tensor"), None),
        ),
        out_specs=(
            P(("dp", "tensor"), None),
            P(("dp", "tensor"), None),
            P(),
            P(None, "tensor"),
            P(None, "tensor"),
            P(None, "tensor"),
            P("tensor", None),
            P(None, "tensor"),
            P(),
            P(),
            P("dp", None, "tensor"),
            P("dp", "tensor", None),
        ),
        check_vma=False,
    )
```

```python
import functools

import jax
import jax.numpy as jnp
import numpy as np
from jax import lax
from jax.experimental import pallas as pl
from jax.experimental.pallas import tpu as pltpu
from jax.sharding import PartitionSpec as P

highest = lax.Precision.HIGHEST
epsilon = 1e-06
apart = 2.0**30
near_reach = 128


def bucket_of(offsets, bucket_count):
    half_count = bucket_count // 2
    exact_count = half_count // 2
    upward = (offsets > 0).astype(np.int32) * half_count
    distance = np.abs(offsets)
    scaled = (
        np.log(np.maximum(distance, 1) / exact_count)
        / np.log(128 / exact_count)
        * (half_count - exact_count)
    )
    distant = np.minimum(exact_count + np.floor(scaled).astype(np.int32), half_count - 1)
    return (upward + np.where(distance < exact_count, distance, distant)).astype(np.int32)


def rounded(values):
    return lax.optimization_barrier(values.astype(jnp.bfloat16)).astype(jnp.float32)


def rms_forward(values, gain_vec):
    scale_row = lax.rsqrt(jnp.mean(values * values, axis=-1, keepdims=True) + epsilon)
    return (values * scale_row * gain_vec, scale_row)


def rms_backward(values, scale_row, gain_vec, normed_grad):
    gain_grad = jnp.sum(normed_grad * values * scale_row, axis=0)
    grad_hat = normed_grad * gain_vec
    row_inner = jnp.mean(grad_hat * values, axis=-1, keepdims=True)
    return (scale_row * (grad_hat - values * scale_row * scale_row * row_inner), gain_grad)


def swap(values, axis_name, bits):
    count = lax.axis_size(axis_name)
    return lax.ppermute(values, axis_name, [(i, i ^ bits) for i in range(count)])


def power_of_two(axis_name):
    count = lax.axis_size(axis_name)
    return count <= 8 and count & (count - 1) == 0


def exchange(chunks):
    return lax.all_to_all(chunks, "dp", split_axis=0, concat_axis=0, tiled=True)


def exchange_four(chunks):
    parts = [swap(chunks[k], "tensor", k) for k in range(1, lax.axis_size("tensor"))]
    return [chunks[0]] + parts


def gather_four(values):
    across = swap(values, "tensor", 2)
    beside = swap(values, "tensor", 1)
    return [values, beside, across, swap(across, "tensor", 1)]


def tie(*arrays):
    return lax.optimization_barrier(arrays)


def pick(stacked, index):
    return lax.dynamic_index_in_dim(stacked, index, axis=0, keepdims=False)


gelu_c = float(np.sqrt(2.0 / np.pi))


def gelu_and_slope(values):
    square = values * values
    bent = jnp.tanh(gelu_c * values * (1.0 + 0.044715 * square))
    half = 0.5 * (1.0 + bent)
    slope = half + 0.5 * values * (1.0 - bent * bent) * (
        gelu_c * (1.0 + 3 * 0.044715 * square)
    )
    return values * half, slope


def dot_nt(left, right):
    return lax.dot_general(
        left, right, (((1,), (1,)), ((), ())), preferred_element_type=jnp.float32
    )


def dot_nn(left, right):
    return lax.dot_general(
        left, right, (((1,), (0,)), ((), ())), preferred_element_type=jnp.float32
    )


def fill_slab(line_ref, slab_ref, heads, block):
    slab_rows = slab_ref.shape[1]
    near_rows = block + 2 * near_reach
    near_start = (slab_rows - near_rows + block) // 2 - block // 2
    line_len = line_ref.shape[1]
    for h in range(heads):
        line = line_ref[h : h + 1, :]
        rolled = pltpu.roll(
            jnp.broadcast_to(line, (block, line_len)), 0, axis=1, stride=1, stride_axis=0
        )
        slab_ref[h, near_start : near_start + near_rows, :] = rolled[:, block:].T
        slab_ref[h, :near_start, :] = jnp.broadcast_to(line[:, :1], (near_start, block))
        after = near_start + near_rows
        slab_ref[h, after:, :] = jnp.broadcast_to(
            line[:, line_len - 1 :], (slab_rows - after, block)
        )


def forward_kernel(
    heads,
    groups,
    me_ref,
    *refs,
):
    parts = refs[:groups]
    (
        gain_ref,
        wq_ref,
        wk_ref,
        wv_ref,
        line_ref,
        segment_ref,
        normed_ref,
        q_ref,
        k_ref,
        v_ref,
        total_ref,
        attended_t_ref,
    ) = refs[groups : groups + 12]
    outputs_to = refs[groups + 12 : 2 * groups + 12]
    slab_ref, vt_ref, attended_ref = refs[2 * groups + 12 :]
    me = me_ref[0]
    block = parts[0].shape[0]
    local_width = v_ref.shape[1]
    wide = q_ref.shape[1]
    head_size = local_width // heads
    seq_len = groups * block
    fill_slab(line_ref, slab_ref, heads, block)
    lane = lax.broadcasted_iota(jnp.int32, (block, wide), 1)
    for k in range(groups):
        here = pl.ds(pl.multiple_of((k ^ me) * block, block), block)
        part, unused = rms_forward(parts[k][...].astype(jnp.float32), gain_ref[...])
        part = part.astype(jnp.bfloat16)
        normed_ref[k] = part
        mark = lane - local_width == segment_ref[here, :]
        queries = dot_nt(part, wq_ref[...]).astype(jnp.bfloat16).astype(jnp.float32)
        queries = queries * head_size ** (-0.5)
        q_ref[here, :] = jnp.where(mark, -apart, queries).astype(jnp.bfloat16)
        keys = dot_nt(part, wk_ref[...])
        other = jnp.logical_and(lane >= local_width, jnp.logical_not(mark))
        k_ref[here, :] = jnp.where(other, 1.0, keys).astype(jnp.bfloat16)
        values = dot_nt(part, wv_ref[...])
        v_ref[here, :] = values.astype(jnp.bfloat16)
        vt_ref[:, here] = values.T.astype(jnp.bfloat16)
    block_lane = lax.broadcasted_iota(jnp.int32, (block, wide), 1)

    def one_block(i, carry):
        here = pl.ds(pl.multiple_of(i * block, block), block)
        offset = pl.multiple_of((groups - 1 - i) * block, block)
        query_blk = q_ref[here, :]
        outputs = []
        for h in range(heads):
            mine = jnp.logical_or(
                jnp.logical_and(block_lane >= h * head_size, block_lane < (h + 1) * head_size),
                block_lane >= local_width,
            )
            query = jnp.where(mine, query_blk, jnp.zeros_like(query_blk))
            scores = dot_nt(k_ref[...], query) + slab_ref[h, pl.ds(offset, seq_len), :]
            peak = jnp.max(scores, axis=0, keepdims=True)
            weights = jnp.exp(scores - peak)
            total = jnp.sum(weights, axis=0, keepdims=True)
            out = dot_nn(
                vt_ref[h * head_size : (h + 1) * head_size, :], weights.astype(jnp.bfloat16)
            )
            outputs.append(out * (1.0 / total))
            total_ref[h : h + 1, here] = peak + jnp.log(total)
        outputs = jnp.concatenate(outputs, axis=0)
        attended_t_ref[:, here] = outputs
        attended_ref[i ^ me] = outputs.T.astype(jnp.bfloat16)
        return carry

    lax.fori_loop(0, groups, one_block, 0)
    for k, output in enumerate(outputs_to):
        output[...] = attended_ref[k]


def backward_kernel(
    heads,
    groups,
    me_ref,
    q_ref,
    k_ref,
    v_ref,
    total_ref,
    line_ref,
    attended_t_ref,
    wq_ref,
    wk_ref,
    wv_ref,
    normed_ref,
    gain_ref,
    *refs,
):
    grads_in = refs[:groups]
    (
        weight_ref,
        *model_refs,
        gain_grad_ref,
        near_ref,
        far_ref,
        slab_ref,
        diag_ref,
        kt_ref,
        qt_ref,
        out_ref,
        out_t_ref,
        inner_ref,
        p_ref,
        ds_ref,
        grad_t_ref,
    ) = refs[groups:]
    me = me_ref[0]
    seq_len, local_width = v_ref.shape
    wide = q_ref.shape[1]
    head_size = local_width // heads
    block = seq_len // groups
    fill_slab(line_ref, slab_ref, heads, block)
    diag_ref[...] = jnp.zeros_like(diag_ref)
    for k in range(groups):
        here = pl.ds(pl.multiple_of((k ^ me) * block, block), block)
        grads = grads_in[k][...]
        out_ref[here, :] = grads
        grads_t = grads.astype(jnp.float32).T
        out_t_ref[:, here] = grads_t.astype(jnp.bfloat16)
        products = grads_t * attended_t_ref[:, here]
        for h in range(heads):
            inner_ref[h : h + 1, here] = jnp.sum(
                products[h * head_size : (h + 1) * head_size], axis=0, keepdims=True
            )
        kt_ref[:, here] = k_ref[here, :].astype(jnp.float32).T.astype(jnp.bfloat16)
        qt_ref[:, here] = q_ref[here, :].astype(jnp.float32).T.astype(jnp.bfloat16)
    wide_lane = lax.broadcasted_iota(jnp.int32, (block, wide), 1)
    lane = lax.broadcasted_iota(jnp.int32, (block, local_width), 1)
    for h in range(heads):
        low, high = h * head_size, (h + 1) * head_size
        mine = jnp.logical_or(
            jnp.logical_and(wide_lane >= low, wide_lane < high), wide_lane >= local_width
        )
        head_lanes = jnp.logical_and(lane >= low, lane < high)

        def one_block(i, carry):
            here = pl.ds(pl.multiple_of(i * block, block), block)
            offset = pl.multiple_of((groups - 1 - i) * block, block)
            query_blk = q_ref[here, :]
            query = jnp.where(mine, query_blk, jnp.zeros_like(query_blk))
            grad_blk = out_ref[here, :]
            grad = jnp.where(head_lanes, grad_blk, jnp.zeros_like(grad_blk))
            scores = dot_nt(k_ref[...], query) + slab_ref[h, pl.ds(offset, seq_len), :]
            probs = jnp.exp(scores - total_ref[h : h + 1, here])
            prob_grad = dot_nt(v_ref[...], grad)
            score_grad = probs * (prob_grad - inner_ref[h : h + 1, here])
            score_low = score_grad.astype(jnp.bfloat16)
            p_ref[:, here] = probs.astype(jnp.bfloat16)
            ds_ref[:, here] = score_low
            diag_ref[h, pl.ds(offset, seq_len), :] += score_grad
            query_grad = dot_nn(kt_ref[low:high, :], score_low) * head_size ** (-0.5)
            grad_t_ref[low:high, here] = query_grad.astype(jnp.bfloat16)
            return carry

        lax.fori_loop(0, groups, one_block, 0)
        grad_t_ref[local_width + low : local_width + high, :] = dot_nt(
            qt_ref[low:high, :], ds_ref[...]
        ).astype(jnp.bfloat16)
        grad_t_ref[2 * local_width + low : 2 * local_width + high, :] = dot_nt(
            out_t_ref[low:high, :], p_ref[...]
        ).astype(jnp.bfloat16)
    weight_grad = jnp.zeros(weight_ref.shape, jnp.float32)
    gain_grad = jnp.zeros(gain_grad_ref.shape, jnp.float32)
    for k in range(groups):
        here = pl.ds(pl.multiple_of((k ^ me) * block, block), block)
        blk = grad_t_ref[:, here]
        weight_grad += dot_nn(blk, normed_ref[k])
        model = jnp.zeros(model_refs[0].shape, jnp.float32)
        for part, w_ref in enumerate((wq_ref, wk_ref, wv_ref)):
            piece = blk[part * local_width : (part + 1) * local_width, :]
            model += dot_nn(piece.astype(jnp.float32).T.astype(jnp.bfloat16), w_ref[...])
        model_refs[k][...] = model.astype(jnp.bfloat16)
        gain_grad += jnp.sum(model * normed_ref[k].astype(jnp.float32), axis=0, keepdims=True)
    gain_grad_ref[...] = gain_grad / gain_ref[...]
    weight_ref[...] = weight_grad.astype(jnp.bfloat16)
    slab_rows = diag_ref.shape[1]
    near_rows = block + 2 * near_reach
    near_start = (slab_rows - near_rows) // 2
    line_len = line_ref.shape[1]
    row_id = lax.broadcasted_iota(jnp.int32, (block, line_len), 0)
    for h in range(heads):
        near = diag_ref[h, near_start : near_start + near_rows, :].T
        near = jnp.concatenate([jnp.zeros((block, line_len - near_rows), jnp.float32), near], axis=1)
        bit = 1
        while bit < block:
            near = jnp.where(
                (row_id // bit) % 2 == 1, pltpu.roll(near, line_len - bit, axis=1), near
            )
            bit *= 2
        near_ref[h : h + 1, :] = jnp.sum(near, axis=0, keepdims=True)
        far_ref[h : h + 1, :] = jnp.sum(diag_ref[h, :near_start, :], axis=0, keepdims=True)
        far_ref[heads + h : heads + h + 1, :] = jnp.sum(
            diag_ref[h, near_start + near_rows :, :], axis=0, keepdims=True
        )


def output_kernel(groups, *refs):
    attended, weights = refs[:groups], refs[groups : 2 * groups]
    hidden_ref, gain_ref, position_ref, grad_ref, middle_ref, normed_ref, send_ref = refs[
        2 * groups :
    ]
    middle = hidden_ref[...].astype(jnp.float32)
    for part, weight in zip(attended, weights):
        middle += dot_nn(part[...], weight[...])
    middle_ref[...] = middle
    normed, unused = rms_forward(middle, gain_ref[...])
    normed = normed.astype(jnp.bfloat16)
    normed_ref[...] = normed
    shape = (send_ref.shape[0], middle.shape[0])
    here = lax.broadcasted_iota(jnp.int32, shape, 0) == position_ref[...]
    here = here.astype(jnp.bfloat16)
    width = middle.shape[1]
    send_ref[:, :width] = dot_nn(here, normed).astype(jnp.bfloat16)
    send_ref[:, width:] = dot_nn(here, grad_ref[...]).astype(jnp.bfloat16)


def token_kernel(
    groups, back_ref, position_ref, middle_ref, gain_ref, grad_ref, *refs
):
    weights, attended = refs[:groups], refs[groups : 2 * groups]
    total_ref, gain_grad_ref, *blocks = refs[2 * groups : 3 * groups + 2]
    outputs = refs[3 * groups + 2 :]
    shape = (middle_ref.shape[0], back_ref.shape[0])
    here = lax.broadcasted_iota(jnp.int32, shape, 1) == position_ref[...]
    normed_grad = dot_nn(here.astype(jnp.bfloat16), back_ref[...])
    middle = middle_ref[...]
    scale = lax.rsqrt(jnp.mean(middle * middle, axis=-1, keepdims=True) + epsilon)
    gain_grad_ref[...] = jnp.sum(normed_grad * middle * scale, axis=0, keepdims=True)
    hat = normed_grad * gain_ref[...]
    inner = jnp.mean(hat * middle, axis=-1, keepdims=True)
    total = grad_ref[...].astype(jnp.float32) + scale * (hat - middle * scale * scale * inner)
    total_ref[...] = total
    low = total.astype(jnp.bfloat16)
    for k, (weight, part, output) in enumerate(zip(weights, attended, outputs)):
        output[...] = dot_nt(low, weight[...]).astype(jnp.bfloat16)
        weight_grad = dot_nn(part[...].astype(jnp.float32).T.astype(jnp.bfloat16), low)
        blocks[k][...] = weight_grad.astype(blocks[k].dtype)


def router_of(rows, router):
    logits = lax.dot_general(
        rows.astype(jnp.float32),
        router,
        (((1,), (1,)), ((), ())),
        precision=highest,
        preferred_element_type=jnp.float32,
    )
    raised = jnp.exp(logits - jnp.max(logits, axis=-1, keepdims=True))
    return raised / jnp.sum(raised, axis=-1, keepdims=True)


def layer_kernel(
    returned_ref, position_ref, route_ref, middle_ref, normed_ref, router_ref, output_ref
):
    probs = router_of(normed_ref[...], router_ref[...])
    chosen = lax.broadcasted_iota(jnp.int32, probs.shape, 1) == route_ref[...]
    gate = jnp.sum(jnp.where(chosen, probs, 0.0), axis=-1, keepdims=True)
    shape = (middle_ref.shape[0], returned_ref.shape[0])
    here = lax.broadcasted_iota(jnp.int32, shape, 1) == position_ref[...]
    produced = dot_nn(here.astype(jnp.bfloat16), returned_ref[...])
    output_ref[...] = (middle_ref[...] + gate * produced).astype(jnp.bfloat16)


def near_kernel(
    me_ref,
    own_ref,
    beside_ref,
    router_ref,
    up_ref,
    down_ref,
    produced_ref,
    rows_ref,
    active_ref,
    pre_grad_ref,
    gated_ref,
    probs_ref,
):
    me = me_ref[0]
    slots = own_ref.shape[0]
    width = up_ref.shape[0]
    for k, both_ref in enumerate((own_ref, beside_ref)):
        here = slice(k * slots, (k + 1) * slots)
        rows = both_ref[:, :width]
        probs = router_of(rows, router_ref[...])
        if k == 0:
            probs_ref[...] = probs
        chosen = lax.broadcasted_iota(jnp.int32, probs.shape, 1) == me
        gate = jnp.sum(jnp.where(chosen, probs, 0.0), axis=-1, keepdims=True)
        gated = (gate * both_ref[:, width:].astype(jnp.float32)).astype(jnp.bfloat16)
        gated_ref[here, :] = gated
        active, slope = gelu_and_slope(dot_nn(rows, up_ref[...]))
        active = active.astype(jnp.bfloat16)
        active_ref[here, :] = active
        produced_ref[here, :] = dot_nn(active, down_ref[...]).astype(jnp.bfloat16)
        active_grad = dot_nt(gated, down_ref[...]).astype(jnp.bfloat16).astype(jnp.float32)
        pre_grad = (active_grad * slope).astype(jnp.bfloat16)
        pre_grad_ref[here, :] = pre_grad
        rows_ref[here, :] = dot_nt(pre_grad, up_ref[...]).astype(jnp.bfloat16)


def far_kernel(
    own_ref,
    beside_ref,
    gated_ref,
    up_ref,
    early_ref,
    late_ref,
    produced_in_ref,
    rows_in_ref,
    produced_ref,
    produced_other_ref,
    rows_ref,
    rows_other_ref,
    active_ref,
    pre_grad_ref,
):
    slots = own_ref.shape[0]
    cut = early_ref.shape[0]
    for k, row_ref in enumerate((own_ref, beside_ref)):
        here = slice(k * slots, (k + 1) * slots)
        active, slope = gelu_and_slope(dot_nn(row_ref[:, : up_ref.shape[0]], up_ref[...]))
        active = active.astype(jnp.bfloat16)
        active_ref[here, :] = active
        produced = produced_in_ref[here, :].astype(jnp.float32) + dot_nn(active[:, :cut], early_ref[...])
        produced = produced + dot_nn(active[:, cut:], late_ref[...])
        gated = gated_ref[here, :]
        active_grad = jnp.concatenate(
            [dot_nt(gated, early_ref[...]), dot_nt(gated, late_ref[...])], axis=1
        )
        active_grad = active_grad.astype(jnp.bfloat16).astype(jnp.float32)
        pre_grad = (active_grad * slope).astype(jnp.bfloat16)
        pre_grad_ref[here, :] = pre_grad
        back = rows_in_ref[here, :].astype(jnp.float32) + dot_nt(pre_grad, up_ref[...])
        if k == 0:
            produced_ref[...] = produced.astype(jnp.bfloat16)
            rows_ref[...] = back.astype(jnp.bfloat16)
        else:
            produced_other_ref[...] = produced.astype(jnp.bfloat16)
            rows_other_ref[...] = back.astype(jnp.bfloat16)


def finish_kernel(
    me_ref,
    produced_in_ref,
    produced_came_ref,
    rows_in_ref,
    rows_came_ref,
    own_ref,
    probs_ref,
    router_ref,
    produced_ref,
    back_ref,
    router_grad_ref,
):
    me = me_ref[0]
    produced = produced_in_ref[...].astype(jnp.float32) + produced_came_ref[...].astype(jnp.float32)
    produced = produced.astype(jnp.bfloat16)
    produced_ref[...] = produced
    width = produced.shape[1]
    gate_grad = jnp.sum(
        own_ref[:, width:].astype(jnp.float32) * produced.astype(jnp.float32), axis=-1, keepdims=True
    )
    probs = probs_ref[...]
    chosen = (lax.broadcasted_iota(jnp.int32, probs.shape, 1) == me).astype(jnp.float32)
    gate = jnp.sum(chosen * probs, axis=-1, keepdims=True)
    logit_grad = probs * (chosen - gate) * gate_grad
    back = rows_in_ref[...].astype(jnp.float32) + rows_came_ref[...].astype(jnp.float32)
    back = back.astype(jnp.bfloat16).astype(jnp.float32)
    term = lax.dot_general(
        logit_grad,
        router_ref[...],
        (((1,), (0,)), ((), ())),
        precision=highest,
        preferred_element_type=jnp.float32,
    )
    back_ref[...] = (back + term).astype(jnp.bfloat16)
    router_grad_ref[...] = lax.dot_general(
        logit_grad.T,
        own_ref[:, :width].astype(jnp.float32),
        (((1,), (0,)), ((), ())),
        precision=highest,
        preferred_element_type=jnp.float32,
    )


def run_local(kernel, name, outs, scratch, flops, *arrays, scalar_first=False):
    in_specs = [pl.BlockSpec(memory_space=pltpu.VMEM)] * len(arrays)
    if scalar_first:
        in_specs[0] = pl.BlockSpec(memory_space=pltpu.SMEM)
    return pl.pallas_call(
        kernel,
        out_shape=tuple(jax.ShapeDtypeStruct(shape, kind) for shape, kind in outs),
        in_specs=in_specs,
        out_specs=tuple([pl.BlockSpec(memory_space=pltpu.VMEM)] * len(outs)),
        scratch_shapes=[pltpu.VMEM(shape, kind) for shape, kind in scratch],
        compiler_params=pltpu.CompilerParams(vmem_limit_bytes=60 * 1024 * 1024),
        cost_estimate=pl.CostEstimate(flops=flops, bytes_accessed=0, transcendentals=0),
        name=name,
    )(*arrays)


def per_device(
    hidden_in,
    segment_ids,
    expert_route,
    slot_index,
    norm1_gain,
    w_query,
    w_key,
    w_value,
    w_out,
    rel_bias,
    norm2_gain,
    w_router,
    w_up,
    w_down,
    out_grad,
):
    low, full = jnp.bfloat16, jnp.float32
    row_count, model_width = hidden_in.shape
    experts = w_router.shape[1]
    c_send = 3 * row_count // (2 * experts)
    slots = experts * c_send
    tensor_me = lax.axis_index("tensor").astype(jnp.int32)
    dp_me = lax.axis_index("dp").astype(jnp.int32)
    me, expert_me = tensor_me.reshape(1), dp_me.reshape(1)
    groups = lax.axis_size("tensor")
    seq_len = groups * row_count
    heads_here = rel_bias.shape[1]
    bucket_count = rel_bias.shape[0]
    local_width = w_query.shape[1]
    wide = -(-(local_width + 4) // 128) * 128
    gain_one, gain_two = norm1_gain.reshape(1, -1), norm2_gain.reshape(1, -1)
    router_t = w_router.T
    position = expert_route * c_send + slot_index
    position_row, position_col = position.reshape(1, -1), position.reshape(-1, 1)

    def dispatch(rows):
        return exchange(rows.reshape(experts, c_send, -1)).reshape(slots, -1)

    line_len = 2 * row_count + 2 * near_reach
    line_offsets = np.arange(line_len) - (row_count + near_reach)
    line_buckets = bucket_of(line_offsets, bucket_count)
    lookup = jnp.asarray(
        (line_buckets[:, None] == np.arange(bucket_count)[None, :]).astype(np.float32)
    )
    line = jnp.einsum("rb,bh->hr", lookup, rel_bias, precision=highest)
    wq_t, wk_t, wv_t = w_query.T, w_key.T, w_value.T
    pad = ((0, wide - local_width), (0, 0))
    wq_wide, wk_wide = jnp.pad(wq_t, pad), jnp.pad(wk_t, pad)
    segment_col = segment_ids.reshape(-1, 1)
    up_local, down_local = w_up[0], w_down[0]
    early = down_local.shape[0] // 2
    down_first, down_rest = down_local[:early], down_local[early:]

    hidden_across = swap(hidden_in, "tensor", 2)
    hidden_beside = swap(hidden_in, "tensor", 1)
    (
        hidden_across,
        line,
        wq_wide,
        wk_wide,
        segment_col,
        w_out_here,
        down_first,
        down_rest,
        position_row,
        position_col,
    ) = tie(
        hidden_across,
        line,
        wq_wide,
        wk_wide,
        segment_col,
        w_out,
        down_first,
        down_rest,
        position_row,
        position_col,
    )
    hidden_four = [hidden_in, hidden_beside, hidden_across, swap(hidden_across, "tensor", 1)]
    w_out_across = swap(w_out_here, "tensor", 2)
    w_out_beside = swap(w_out_here, "tensor", 1)
    down_early = swap(down_first, "tensor", 2)
    attention_flops = seq_len * seq_len * wide * heads_here * 14
    slab = ((heads_here, 2 * seq_len - row_count, row_count), full)
    normed_four, queries, keys_all, values_all, totals, attended_t, *attended_four = run_local(
        functools.partial(forward_kernel, heads_here, groups),
        "attention_forward",
        [
            ((groups, row_count, model_width), low),
            ((seq_len, wide), low),
            ((seq_len, wide), low),
            ((seq_len, local_width), low),
            ((heads_here, seq_len), full),
            ((local_width, seq_len), full),
        ]
        + [((row_count, local_width), low)] * groups,
        [slab, ((local_width, seq_len), low), ((groups, row_count, local_width), low)],
        attention_flops,
        me,
        *hidden_four,
        gain_one,
        wq_wide,
        wk_wide,
        wv_t,
        line,
        segment_col,
        scalar_first=True,
    )
    *attended_four, w_out_across, w_out_beside, down_early = tie(
        *attended_four, w_out_across, w_out_beside, down_early
    )
    w_out_four = [w_out_here, w_out_beside, w_out_across, swap(w_out_across, "tensor", 1)]
    attended_here = exchange_four(attended_four)
    *attended_here, up_first, down_rest = tie(*attended_here, up_local, down_rest)
    up_far = swap(up_first, "tensor", 2)
    down_late = swap(down_rest, "tensor", 2)
    middle, normed_two, send_rows = run_local(
        functools.partial(output_kernel, groups),
        "output_projection",
        [
            ((row_count, model_width), full),
            ((row_count, model_width), low),
            ((slots, 2 * model_width), low),
        ],
        [],
        0,
        *attended_here,
        *w_out_four,
        hidden_in,
        gain_two,
        position_row,
        out_grad,
    )
    rows_here = dispatch(send_rows)
    rows_here, up_far = tie(rows_here, up_far)
    rows_beside = swap(rows_here, "tensor", 1)

    both, hidden_here = 2 * slots, up_local.shape[1]
    expert_flops = 0
    produced_near, rows_near, active_near, pre_grad_near, gated, probs = run_local(
        near_kernel,
        "expert_near",
        [
            ((both, model_width), low),
            ((both, model_width), low),
            ((both, hidden_here), low),
            ((both, hidden_here), low),
            ((both, model_width), low),
            ((slots, experts), full),
        ],
        [],
        expert_flops,
        expert_me,
        rows_here,
        rows_beside,
        router_t,
        up_local,
        down_local,
        scalar_first=True,
    )
    rows_near, down_late = tie(rows_near, down_late)
    produced_own, produced_other, rows_own, rows_other, active_far, pre_grad_far = run_local(
        far_kernel,
        "expert_far",
        [
            ((slots, model_width), low),
            ((slots, model_width), low),
            ((slots, model_width), low),
            ((slots, model_width), low),
            ((both, hidden_here), low),
            ((both, hidden_here), low),
        ],
        [],
        expert_flops,
        rows_here,
        rows_beside,
        gated,
        up_far,
        down_early,
        down_late,
        produced_near,
        rows_near,
    )
    produced, rows_back, router_grad = run_local(
        finish_kernel,
        "expert_finish",
        [
            ((slots, model_width), low),
            ((slots, model_width), low),
            ((experts, model_width), full),
        ],
        [],
        0,
        expert_me,
        produced_own,
        swap(produced_other, "tensor", 1),
        rows_own,
        swap(rows_other, "tensor", 1),
        rows_here,
        probs,
        router_t,
        scalar_first=True,
    )

    grads_back = dispatch(rows_back)

    def of_weights(left, right):
        return jnp.einsum("cd,cf->df", left, right, preferred_element_type=full)

    expert_rows = jnp.concatenate([rows_here[:, :model_width], rows_beside[:, :model_width]])
    down_sent = of_weights(active_far, gated).astype(low)
    half = down_sent.shape[0] // 2
    grads_back, produced, down_one, down_two, up_sent, up_near, down_near = tie(
        grads_back,
        produced,
        down_sent[:half],
        down_sent[half:],
        of_weights(expert_rows, pre_grad_far).astype(low),
        of_weights(expert_rows, pre_grad_near),
        of_weights(active_near, gated),
    )
    middle_grad, gain_two_grad, out_own, out_beside, out_across, out_corner, *grad_four = run_local(
        functools.partial(token_kernel, groups),
        "token_backward",
        [
            ((row_count, model_width), full),
            ((1, model_width), full),
            ((local_width, model_width), low),
            ((local_width, model_width), low),
            ((local_width, model_width), low),
            ((local_width, model_width), low),
        ]
        + [((row_count, local_width), low)] * groups,
        [],
        0,
        grads_back,
        position_col,
        middle,
        gain_two,
        out_grad,
        *w_out_four,
        *attended_here,
    )
    grad_four = exchange_four(grad_four)
    out_came = swap(out_beside, "tensor", 1).astype(full)
    out_sent = (out_across.astype(full) + swap(out_corner, "tensor", 1).astype(full)).astype(low)
    *grad_four, out_sent, down_one = tie(*grad_four, out_sent, down_one)
    out_last = swap(out_sent, "tensor", 2)
    down_one = swap(down_one, "tensor", 2)
    grad_four[1], produced = tie(grad_four[1], produced)
    returned = dispatch(produced)

    backward = run_local(
        functools.partial(backward_kernel, heads_here, groups),
        "attention_backward",
        [
            ((3 * local_width, model_width), low),
            ((row_count, model_width), low),
            ((row_count, model_width), low),
            ((row_count, model_width), low),
            ((row_count, model_width), low),
            ((1, model_width), full),
            ((heads_here, line_len), full),
            ((2 * heads_here, row_count), full),
        ],
        [
            slab,
            slab,
            ((wide, seq_len), low),
            ((wide, seq_len), low),
            ((seq_len, local_width), low),
            ((local_width, seq_len), low),
            ((heads_here, seq_len), full),
            ((seq_len, seq_len), low),
            ((seq_len, seq_len), low),
            ((3 * local_width, seq_len), low),
        ],
        0,
        me,
        queries,
        keys_all,
        values_all,
        totals,
        line,
        attended_t,
        wq_t,
        wk_t,
        wv_t,
        normed_four,
        gain_one,
        *grad_four,
        scalar_first=True,
    )
    (
        weight_grad,
        own_part,
        beside_part,
        across_part,
        corner_part,
        gain_one_grad,
        near_grad,
        far_grad,
    ) = backward
    corner_came = swap(corner_part, "tensor", 1).astype(full)
    beside_came = swap(beside_part, "tensor", 1).astype(full)
    across_sent = (across_part.astype(full) + corner_came).astype(low)
    up_one = swap(up_sent[: up_sent.shape[0] // 2], "tensor", 2)
    out_weight_grad = (out_own.astype(full) + out_came + out_last.astype(full)).astype(low)
    dense_rows = 4 * local_width
    count = lax.axis_size("dp")
    dense = jnp.concatenate([weight_grad, out_weight_grad]).reshape(count, -1, model_width)
    dense, returned, down_one = tie(dense, returned, down_one)
    dense = jnp.sum(exchange(dense).astype(full), axis=0).astype(low)

    far_here = jnp.sum(far_grad, axis=1).reshape(2, heads_here)
    rel_grad = jnp.einsum("rb,hr->hb", lookup, near_grad, precision=highest)
    far_place = np.zeros((2, bucket_count), np.float32)
    far_place[0, bucket_count // 2 - 1] = 1.0
    far_place[1, bucket_count - 1] = 1.0
    rel_grad = rel_grad + jnp.sum(far_here[:, :, None] * far_place[:, None, :], axis=0)
    rel_place = (jnp.arange(groups, dtype=jnp.int32) == tensor_me).astype(full)
    rel_wide = rel_place[:, None, None] * rel_grad[None]
    flat = jnp.concatenate(
        [
            gain_one_grad.reshape(-1),
            gain_two_grad.reshape(-1),
            router_grad.reshape(-1),
            rel_wide.reshape(-1),
        ]
    )
    flat_rows = -(-flat.shape[0] // (16 * model_width)) * 16
    flat = flat + swap(flat, "tensor", 2)
    flat = flat + swap(flat, "tensor", 1)
    flat = jnp.pad(flat, (0, flat_rows * model_width - flat.shape[0]))
    payload = jnp.concatenate([dense, flat.reshape(flat_rows, model_width).astype(low)])
    across = swap(across_sent, "tensor", 2)
    rest = jnp.concatenate([up_sent[up_sent.shape[0] // 2 :], down_two])
    payload, returned, up_one, across, rest = tie(payload, returned, up_one, across, rest)
    rest = swap(rest, "tensor", 2)
    payload = exchange(jnp.broadcast_to(payload[None], (count, *payload.shape)))
    dense, flat = payload[:, : dense_rows // count], payload[:, dense_rows // count :]
    dense = dense.reshape(dense_rows, model_width)

    normed_grad = rounded(own_part.astype(full) + beside_came + across.astype(full))
    inputs_f = hidden_in.astype(full)
    unused, scale_one = rms_forward(inputs_f, norm1_gain)
    input_part, unused = rms_backward(inputs_f, scale_one, norm1_gain, normed_grad)
    input_grad = middle_grad + input_part
    (layer_out,) = run_local(
        layer_kernel,
        "layer_output",
        [((row_count, model_width), low)],
        [],
        12 * 10**9,
        returned,
        position_col,
        expert_route.reshape(-1, 1),
        middle,
        normed_two,
        router_t,
    )
    layer_out, rest = tie(layer_out, rest)
    up_grad = up_near + jnp.concatenate([up_one, rest[:half]]).astype(full)
    down_grad = down_near + jnp.concatenate([down_one, rest[half:]]).astype(full)
    dense = dense.astype(full)
    flat = jnp.sum(flat.astype(full), axis=0).reshape(-1)
    gain_one_grad = flat[:model_width]
    gain_two_grad = flat[model_width : 2 * model_width]
    split = 2 * model_width + model_width * experts
    router_grad = flat[2 * model_width : split].reshape(experts, model_width).T
    rel_all = flat[split : split + groups * heads_here * bucket_count]
    rel_grad = pick(rel_all.reshape(groups, heads_here, bucket_count), tensor_me).T
    return (
        layer_out,
        input_grad,
        gain_one_grad,
        dense[:local_width].T,
        dense[local_width : 2 * local_width].T,
        dense[2 * local_width : 3 * local_width].T,
        dense[3 * local_width :],
        rel_grad,
        gain_two_grad,
        router_grad,
        up_grad[None],
        down_grad[None],
    )


def solution(mesh):
    return jax.shard_map(
        per_device,
        mesh=mesh,
        in_specs=(
            P(("dp", "tensor"), None),
            P("dp", None),
            P(("dp", "tensor")),
            P(("dp", "tensor")),
            P(),
            P(None, "tensor"),
            P(None, "tensor"),
            P(None, "tensor"),
            P("tensor", None),
            P(None, "tensor"),
            P(),
            P(),
            P("dp", None, "tensor"),
            P("dp", "tensor", None),
            P(("dp", "tensor"), None),
        ),
        out_specs=(
            P(("dp", "tensor"), None),
            P(("dp", "tensor"), None),
            P(),
            P(None, "tensor"),
            P(None, "tensor"),
            P(None, "tensor"),
            P("tensor", None),
            P(None, "tensor"),
            P(),
            P(),
            P("dp", None, "tensor"),
            P("dp", "tensor", None),
        ),
        check_vma=False,
    )
```

```python
import functools

import jax
import jax.numpy as jnp
import numpy as np
from jax import lax
from jax.experimental import pallas as pl
from jax.experimental.pallas import tpu as pltpu
from jax.sharding import PartitionSpec as P

highest = lax.Precision.HIGHEST
epsilon = 1e-06
apart = 2.0**30
near_reach = 128


def bucket_of(offsets, bucket_count):
    half_count = bucket_count // 2
    exact_count = half_count // 2
    upward = (offsets > 0).astype(np.int32) * half_count
    distance = np.abs(offsets)
    scaled = (
        np.log(np.maximum(distance, 1) / exact_count)
        / np.log(128 / exact_count)
        * (half_count - exact_count)
    )
    distant = np.minimum(exact_count + np.floor(scaled).astype(np.int32), half_count - 1)
    return (upward + np.where(distance < exact_count, distance, distant)).astype(np.int32)


def rounded(values):
    return lax.optimization_barrier(values.astype(jnp.bfloat16)).astype(jnp.float32)


def rms_forward(values, gain_vec):
    scale_row = lax.rsqrt(jnp.mean(values * values, axis=-1, keepdims=True) + epsilon)
    return (values * scale_row * gain_vec, scale_row)


def rms_backward(values, scale_row, gain_vec, normed_grad):
    gain_grad = jnp.sum(normed_grad * values * scale_row, axis=0)
    grad_hat = normed_grad * gain_vec
    row_inner = jnp.mean(grad_hat * values, axis=-1, keepdims=True)
    return (scale_row * (grad_hat - values * scale_row * scale_row * row_inner), gain_grad)


def swap(values, axis_name, bits):
    count = lax.axis_size(axis_name)
    return lax.ppermute(values, axis_name, [(i, i ^ bits) for i in range(count)])


def power_of_two(axis_name):
    count = lax.axis_size(axis_name)
    return count <= 8 and count & (count - 1) == 0


def exchange(chunks):
    return lax.all_to_all(chunks, "dp", split_axis=0, concat_axis=0, tiled=True)


def exchange_four(chunks):
    parts = [swap(chunks[k], "tensor", k) for k in range(1, lax.axis_size("tensor"))]
    return [chunks[0]] + parts


def gather_four(values):
    across = swap(values, "tensor", 2)
    beside = swap(values, "tensor", 1)
    return [values, beside, across, swap(across, "tensor", 1)]


def tie(*arrays):
    return lax.optimization_barrier(arrays)


def pick(stacked, index):
    return lax.dynamic_index_in_dim(stacked, index, axis=0, keepdims=False)


gelu_c = float(np.sqrt(2.0 / np.pi))


def gelu_and_slope(values):
    square = values * values
    bent = jnp.tanh(gelu_c * values * (1.0 + 0.044715 * square))
    half = 0.5 * (1.0 + bent)
    slope = half + 0.5 * values * (1.0 - bent * bent) * (
        gelu_c * (1.0 + 3 * 0.044715 * square)
    )
    return values * half, slope


def dot_nt(left, right):
    return lax.dot_general(
        left, right, (((1,), (1,)), ((), ())), preferred_element_type=jnp.float32
    )


def dot_nn(left, right):
    return lax.dot_general(
        left, right, (((1,), (0,)), ((), ())), preferred_element_type=jnp.float32
    )


def fill_slab(line_ref, slab_ref, heads, block):
    slab_rows = slab_ref.shape[1]
    near_rows = block + 2 * near_reach
    near_start = (slab_rows - near_rows + block) // 2 - block // 2
    line_len = line_ref.shape[1]
    for h in range(heads):
        line = line_ref[h : h + 1, :]
        rolled = pltpu.roll(
            jnp.broadcast_to(line, (block, line_len)), 0, axis=1, stride=1, stride_axis=0
        )
        slab_ref[h, near_start : near_start + near_rows, :] = rolled[:, block:].T
        slab_ref[h, :near_start, :] = jnp.broadcast_to(line[:, :1], (near_start, block))
        after = near_start + near_rows
        slab_ref[h, after:, :] = jnp.broadcast_to(
            line[:, line_len - 1 :], (slab_rows - after, block)
        )


def key_spans(groups):
    if groups != 4:
        return [(list(range(groups)), groups)]
    return [([1, 2], 4), ([0, 3], 3)]


def over_blocks(groups, block, one_block, unroll):
    for blocks, key_blocks in key_spans(groups):
        low, step = blocks[0], blocks[1] - blocks[0]

        def body(j, carry, low=low, step=step, key_blocks=key_blocks):
            i = low + step * j
            one_block(i, j if key_blocks < groups else 0, key_blocks * block)
            return carry

        lax.fori_loop(0, len(blocks), body, 0, unroll=unroll)


def forward_kernel(
    heads,
    groups,
    me_ref,
    *refs,
):
    parts = refs[:groups]
    (
        gain_ref,
        wq_ref,
        wk_ref,
        wv_ref,
        line_ref,
        segment_ref,
        normed_ref,
        q_ref,
        k_ref,
        v_ref,
        total_ref,
    ) = refs[groups : groups + 11]
    outputs_to = refs[groups + 11 : 2 * groups + 11]
    slab_ref, vt_ref, attended_ref = refs[2 * groups + 11 :]
    me = me_ref[0]
    block = parts[0].shape[0]
    local_width = v_ref.shape[1]
    wide = q_ref.shape[1]
    head_size = local_width // heads
    seq_len = groups * block
    fill_slab(line_ref, slab_ref, heads, block)
    lane = lax.broadcasted_iota(jnp.int32, (block, wide), 1)
    for k in range(groups):
        here = pl.ds(pl.multiple_of((k ^ me) * block, block), block)
        part, unused = rms_forward(parts[k][...].astype(jnp.float32), gain_ref[...])
        part = part.astype(jnp.bfloat16)
        normed_ref[k] = part
        mark = lane - local_width == segment_ref[here, :]
        queries = dot_nt(part, wq_ref[...]).astype(jnp.bfloat16).astype(jnp.float32)
        queries = queries * head_size ** (-0.5)
        q_ref[here, :] = jnp.where(mark, -apart, queries).astype(jnp.bfloat16)
        keys = dot_nt(part, wk_ref[...])
        other = jnp.logical_and(lane >= local_width, jnp.logical_not(mark))
        k_ref[here, :] = jnp.where(other, 1.0, keys).astype(jnp.bfloat16)
        values = dot_nt(part, wv_ref[...])
        v_ref[here, :] = values.astype(jnp.bfloat16)
        vt_ref[:, here] = values.T.astype(jnp.bfloat16)
    block_lane = lax.broadcasted_iota(jnp.int32, (block, wide), 1)

    def one_block(i, first, key_count):
        here = pl.ds(pl.multiple_of(i * block, block), block)
        keys = pl.ds(pl.multiple_of(first * block, block), key_count)
        places = pl.ds(pl.multiple_of((groups - 1 - i + first) * block, block), key_count)
        query_blk = q_ref[here, :]
        outputs = []
        for h in range(heads):
            mine = jnp.logical_or(
                jnp.logical_and(block_lane >= h * head_size, block_lane < (h + 1) * head_size),
                block_lane >= local_width,
            )
            query = jnp.where(mine, query_blk, jnp.zeros_like(query_blk))
            scores = dot_nt(k_ref[keys, :], query) + slab_ref[h, places, :]
            peak = jnp.max(scores, axis=0, keepdims=True)
            weights = jnp.exp(scores - peak)
            total = jnp.sum(weights, axis=0, keepdims=True)
            out = dot_nn(
                vt_ref[h * head_size : (h + 1) * head_size, keys], weights.astype(jnp.bfloat16)
            )
            outputs.append(out * (1.0 / total))
            total_ref[h : h + 1, here] = peak + jnp.log(total)
        outputs = jnp.concatenate(outputs, axis=0)
        attended_ref[i ^ me] = outputs.T.astype(jnp.bfloat16)

    over_blocks(groups, block, one_block, False)
    for k, output in enumerate(outputs_to):
        output[...] = attended_ref[k]


def backward_kernel(
    heads,
    groups,
    me_ref,
    q_ref,
    k_ref,
    v_ref,
    total_ref,
    line_ref,
    wq_ref,
    wk_ref,
    wv_ref,
    normed_ref,
    gain_ref,
    *refs,
):
    grads_in, attended_in = refs[:groups], refs[groups : 2 * groups]
    (
        weight_ref,
        *model_refs,
        gain_grad_ref,
        near_ref,
        far_ref,
        slab_ref,
        diag_ref,
        kt_ref,
        qt_ref,
        out_ref,
        out_t_ref,
        inner_ref,
        p_ref,
        ds_ref,
        grad_t_ref,
    ) = refs[2 * groups :]
    me = me_ref[0]
    seq_len, local_width = v_ref.shape
    wide = q_ref.shape[1]
    head_size = local_width // heads
    block = seq_len // groups
    fill_slab(line_ref, slab_ref, heads, block)
    diag_ref[...] = jnp.zeros_like(diag_ref)
    for k in range(groups):
        here = pl.ds(pl.multiple_of((k ^ me) * block, block), block)
        grads = grads_in[k][...]
        out_ref[here, :] = grads
        grads = grads.astype(jnp.float32)
        out_t_ref[:, here] = grads.T.astype(jnp.bfloat16)
        products = (grads * attended_in[k][...].astype(jnp.float32)).T
        for h in range(heads):
            inner_ref[h : h + 1, here] = jnp.sum(
                products[h * head_size : (h + 1) * head_size], axis=0, keepdims=True
            )
        kt_ref[:, here] = k_ref[here, :].astype(jnp.float32).T.astype(jnp.bfloat16)
        qt_ref[:, here] = q_ref[here, :].astype(jnp.float32).T.astype(jnp.bfloat16)
    wide_lane = lax.broadcasted_iota(jnp.int32, (block, wide), 1)
    lane = lax.broadcasted_iota(jnp.int32, (block, local_width), 1)
    for h in range(heads):
        low, high = h * head_size, (h + 1) * head_size
        mine = jnp.logical_or(
            jnp.logical_and(wide_lane >= low, wide_lane < high), wide_lane >= local_width
        )
        head_lanes = jnp.logical_and(lane >= low, lane < high)

        def one_block(i, first, key_count, low=low, high=high, mine=mine, head_lanes=head_lanes):
            here = pl.ds(pl.multiple_of(i * block, block), block)
            keys = pl.ds(pl.multiple_of(first * block, block), key_count)
            places = pl.ds(pl.multiple_of((groups - 1 - i + first) * block, block), key_count)
            query_blk = q_ref[here, :]
            query = jnp.where(mine, query_blk, jnp.zeros_like(query_blk))
            grad_blk = out_ref[here, :]
            grad = jnp.where(head_lanes, grad_blk, jnp.zeros_like(grad_blk))
            scores = dot_nt(k_ref[keys, :], query) + slab_ref[h, places, :]
            probs = jnp.exp(scores - total_ref[h : h + 1, here])
            prob_grad = dot_nt(v_ref[keys, :], grad)
            score_grad = probs * (prob_grad - inner_ref[h : h + 1, here])
            score_low = score_grad.astype(jnp.bfloat16)
            p_ref[keys, here] = probs.astype(jnp.bfloat16)
            ds_ref[keys, here] = score_low
            diag_ref[h, places, :] += score_grad
            query_grad = dot_nn(kt_ref[low:high, keys], score_low) * head_size ** (-0.5)
            grad_t_ref[low:high, here] = query_grad.astype(jnp.bfloat16)

        over_blocks(groups, block, one_block, True)
        for j in range(groups):
            keys = slice(j * block, (j + 1) * block)
            first, last = (max(0, j - 2), min(groups, j + 3)) if groups == 4 else (0, groups)
            meet = slice(first * block, last * block)
            grad_t_ref[local_width + low : local_width + high, keys] = dot_nt(
                qt_ref[low:high, meet], ds_ref[keys, meet]
            ).astype(jnp.bfloat16)
            grad_t_ref[2 * local_width + low : 2 * local_width + high, keys] = dot_nt(
                out_t_ref[low:high, meet], p_ref[keys, meet]
            ).astype(jnp.bfloat16)
    weight_grad = jnp.zeros(weight_ref.shape, jnp.float32)
    gain_grad = jnp.zeros(gain_grad_ref.shape, jnp.float32)
    for k in range(groups):
        here = pl.ds(pl.multiple_of((k ^ me) * block, block), block)
        blk = grad_t_ref[:, here]
        weight_grad += dot_nn(blk, normed_ref[k])
        model = jnp.zeros(model_refs[0].shape, jnp.float32)
        for part, w_ref in enumerate((wq_ref, wk_ref, wv_ref)):
            piece = blk[part * local_width : (part + 1) * local_width, :]
            model += dot_nn(piece.astype(jnp.float32).T.astype(jnp.bfloat16), w_ref[...])
        model_refs[k][...] = model.astype(jnp.bfloat16)
        gain_grad += jnp.sum(model * normed_ref[k].astype(jnp.float32), axis=0, keepdims=True)
    gain_grad_ref[...] = gain_grad / gain_ref[...]
    weight_ref[...] = weight_grad.astype(jnp.bfloat16)
    slab_rows = diag_ref.shape[1]
    near_rows = block + 2 * near_reach
    near_start = (slab_rows - near_rows) // 2
    line_len = line_ref.shape[1]
    row_id = lax.broadcasted_iota(jnp.int32, (block, line_len), 0)
    for h in range(heads):
        near = diag_ref[h, near_start : near_start + near_rows, :].T
        near = jnp.concatenate([jnp.zeros((block, line_len - near_rows), jnp.float32), near], axis=1)
        bit = 1
        while bit < block:
            near = jnp.where(
                (row_id // bit) % 2 == 1, pltpu.roll(near, line_len - bit, axis=1), near
            )
            bit *= 2
        near_ref[h : h + 1, :] = jnp.sum(near, axis=0, keepdims=True)
        far_ref[h : h + 1, :] = jnp.sum(diag_ref[h, :near_start, :], axis=0, keepdims=True)
        far_ref[heads + h : heads + h + 1, :] = jnp.sum(
            diag_ref[h, near_start + near_rows :, :], axis=0, keepdims=True
        )


def output_kernel(groups, *refs):
    attended, weights = refs[:groups], refs[groups : 2 * groups]
    hidden_ref, gain_ref, position_ref, grad_ref, middle_ref, normed_ref, send_ref = refs[
        2 * groups :
    ]
    middle = hidden_ref[...].astype(jnp.float32)
    for part, weight in zip(attended, weights):
        middle += dot_nn(part[...], weight[...])
    middle_ref[...] = middle
    normed, unused = rms_forward(middle, gain_ref[...])
    normed = normed.astype(jnp.bfloat16)
    normed_ref[...] = normed
    shape = (send_ref.shape[0], middle.shape[0])
    here = lax.broadcasted_iota(jnp.int32, shape, 0) == position_ref[...]
    here = here.astype(jnp.bfloat16)
    width = middle.shape[1]
    send_ref[:, :width] = dot_nn(here, normed).astype(jnp.bfloat16)
    send_ref[:, width:] = dot_nn(here, grad_ref[...]).astype(jnp.bfloat16)


def token_kernel(
    groups, back_ref, position_ref, middle_ref, gain_ref, grad_ref, *refs
):
    weights, attended = refs[:groups], refs[groups : 2 * groups]
    total_ref, gain_grad_ref, *blocks = refs[2 * groups : 3 * groups + 2]
    outputs = refs[3 * groups + 2 :]
    shape = (middle_ref.shape[0], back_ref.shape[0])
    here = lax.broadcasted_iota(jnp.int32, shape, 1) == position_ref[...]
    normed_grad = dot_nn(here.astype(jnp.bfloat16), back_ref[...])
    middle = middle_ref[...]
    scale = lax.rsqrt(jnp.mean(middle * middle, axis=-1, keepdims=True) + epsilon)
    gain_grad_ref[...] = jnp.sum(normed_grad * middle * scale, axis=0, keepdims=True)
    hat = normed_grad * gain_ref[...]
    inner = jnp.mean(hat * middle, axis=-1, keepdims=True)
    total = grad_ref[...].astype(jnp.float32) + scale * (hat - middle * scale * scale * inner)
    total_ref[...] = total
    low = total.astype(jnp.bfloat16)
    for k, (weight, part, output) in enumerate(zip(weights, attended, outputs)):
        output[...] = dot_nt(low, weight[...]).astype(jnp.bfloat16)
        weight_grad = dot_nn(part[...].astype(jnp.float32).T.astype(jnp.bfloat16), low)
        blocks[k][...] = weight_grad.astype(blocks[k].dtype)


def router_of(rows, router):
    logits = lax.dot_general(
        rows.astype(jnp.float32),
        router,
        (((1,), (1,)), ((), ())),
        precision=highest,
        preferred_element_type=jnp.float32,
    )
    raised = jnp.exp(logits - jnp.max(logits, axis=-1, keepdims=True))
    return raised / jnp.sum(raised, axis=-1, keepdims=True)


def layer_kernel(
    returned_ref, position_ref, route_ref, middle_ref, normed_ref, router_ref, output_ref
):
    probs = router_of(normed_ref[...], router_ref[...])
    chosen = lax.broadcasted_iota(jnp.int32, probs.shape, 1) == route_ref[...]
    gate = jnp.sum(jnp.where(chosen, probs, 0.0), axis=-1, keepdims=True)
    shape = (middle_ref.shape[0], returned_ref.shape[0])
    here = lax.broadcasted_iota(jnp.int32, shape, 1) == position_ref[...]
    produced = dot_nn(here.astype(jnp.bfloat16), returned_ref[...])
    output_ref[...] = (middle_ref[...] + gate * produced).astype(jnp.bfloat16)


def near_kernel(
    me_ref,
    own_ref,
    beside_ref,
    router_ref,
    up_ref,
    down_ref,
    produced_ref,
    rows_ref,
    active_ref,
    pre_grad_ref,
    gated_ref,
    probs_ref,
):
    me = me_ref[0]
    slots = own_ref.shape[0]
    width = up_ref.shape[0]
    for k, both_ref in enumerate((own_ref, beside_ref)):
        here = slice(k * slots, (k + 1) * slots)
        rows = both_ref[:, :width]
        probs = router_of(rows, router_ref[...])
        if k == 0:
            probs_ref[...] = probs
        chosen = lax.broadcasted_iota(jnp.int32, probs.shape, 1) == me
        gate = jnp.sum(jnp.where(chosen, probs, 0.0), axis=-1, keepdims=True)
        gated = (gate * both_ref[:, width:].astype(jnp.float32)).astype(jnp.bfloat16)
        gated_ref[here, :] = gated
        active, slope = gelu_and_slope(dot_nn(rows, up_ref[...]))
        active = active.astype(jnp.bfloat16)
        active_ref[here, :] = active
        produced_ref[here, :] = dot_nn(active, down_ref[...]).astype(jnp.bfloat16)
        active_grad = dot_nt(gated, down_ref[...]).astype(jnp.bfloat16).astype(jnp.float32)
        pre_grad = (active_grad * slope).astype(jnp.bfloat16)
        pre_grad_ref[here, :] = pre_grad
        rows_ref[here, :] = dot_nt(pre_grad, up_ref[...]).astype(jnp.bfloat16)


def far_kernel(
    own_ref,
    beside_ref,
    gated_ref,
    up_ref,
    early_ref,
    late_ref,
    produced_in_ref,
    rows_in_ref,
    produced_ref,
    produced_other_ref,
    rows_ref,
    rows_other_ref,
    active_ref,
    pre_grad_ref,
):
    slots = own_ref.shape[0]
    cut = early_ref.shape[0]
    for k, row_ref in enumerate((own_ref, beside_ref)):
        here = slice(k * slots, (k + 1) * slots)
        active, slope = gelu_and_slope(dot_nn(row_ref[:, : up_ref.shape[0]], up_ref[...]))
        active = active.astype(jnp.bfloat16)
        active_ref[here, :] = active
        produced = produced_in_ref[here, :].astype(jnp.float32) + dot_nn(active[:, :cut], early_ref[...])
        produced = produced + dot_nn(active[:, cut:], late_ref[...])
        gated = gated_ref[here, :]
        active_grad = jnp.concatenate(
            [dot_nt(gated, early_ref[...]), dot_nt(gated, late_ref[...])], axis=1
        )
        active_grad = active_grad.astype(jnp.bfloat16).astype(jnp.float32)
        pre_grad = (active_grad * slope).astype(jnp.bfloat16)
        pre_grad_ref[here, :] = pre_grad
        back = rows_in_ref[here, :].astype(jnp.float32) + dot_nt(pre_grad, up_ref[...])
        if k == 0:
            produced_ref[...] = produced.astype(jnp.bfloat16)
            rows_ref[...] = back.astype(jnp.bfloat16)
        else:
            produced_other_ref[...] = produced.astype(jnp.bfloat16)
            rows_other_ref[...] = back.astype(jnp.bfloat16)


def finish_kernel(
    me_ref,
    produced_in_ref,
    produced_came_ref,
    rows_in_ref,
    rows_came_ref,
    own_ref,
    probs_ref,
    router_ref,
    produced_ref,
    back_ref,
    router_grad_ref,
):
    me = me_ref[0]
    produced = produced_in_ref[...].astype(jnp.float32) + produced_came_ref[...].astype(jnp.float32)
    produced = produced.astype(jnp.bfloat16)
    produced_ref[...] = produced
    width = produced.shape[1]
    gate_grad = jnp.sum(
        own_ref[:, width:].astype(jnp.float32) * produced.astype(jnp.float32), axis=-1, keepdims=True
    )
    probs = probs_ref[...]
    chosen = (lax.broadcasted_iota(jnp.int32, probs.shape, 1) == me).astype(jnp.float32)
    gate = jnp.sum(chosen * probs, axis=-1, keepdims=True)
    logit_grad = probs * (chosen - gate) * gate_grad
    back = rows_in_ref[...].astype(jnp.float32) + rows_came_ref[...].astype(jnp.float32)
    back = back.astype(jnp.bfloat16).astype(jnp.float32)
    term = lax.dot_general(
        logit_grad,
        router_ref[...],
        (((1,), (0,)), ((), ())),
        precision=highest,
        preferred_element_type=jnp.float32,
    )
    back_ref[...] = (back + term).astype(jnp.bfloat16)
    router_grad_ref[...] = lax.dot_general(
        logit_grad.T,
        own_ref[:, :width].astype(jnp.float32),
        (((1,), (0,)), ((), ())),
        precision=highest,
        preferred_element_type=jnp.float32,
    )


def run_local(kernel, name, outs, scratch, flops, *arrays, scalar_first=False):
    in_specs = [pl.BlockSpec(memory_space=pltpu.VMEM)] * len(arrays)
    if scalar_first:
        in_specs[0] = pl.BlockSpec(memory_space=pltpu.SMEM)
    return pl.pallas_call(
        kernel,
        out_shape=tuple(jax.ShapeDtypeStruct(shape, kind) for shape, kind in outs),
        in_specs=in_specs,
        out_specs=tuple([pl.BlockSpec(memory_space=pltpu.VMEM)] * len(outs)),
        scratch_shapes=[pltpu.VMEM(shape, kind) for shape, kind in scratch],
        compiler_params=pltpu.CompilerParams(vmem_limit_bytes=60 * 1024 * 1024),
        cost_estimate=pl.CostEstimate(flops=flops, bytes_accessed=0, transcendentals=0),
        name=name,
    )(*arrays)


def per_device(
    hidden_in,
    segment_ids,
    expert_route,
    slot_index,
    norm1_gain,
    w_query,
    w_key,
    w_value,
    w_out,
    rel_bias,
    norm2_gain,
    w_router,
    w_up,
    w_down,
    out_grad,
):
    low, full = jnp.bfloat16, jnp.float32
    row_count, model_width = hidden_in.shape
    experts = w_router.shape[1]
    c_send = 3 * row_count // (2 * experts)
    slots = experts * c_send
    tensor_me = lax.axis_index("tensor").astype(jnp.int32)
    dp_me = lax.axis_index("dp").astype(jnp.int32)
    me, expert_me = tensor_me.reshape(1), dp_me.reshape(1)
    groups = lax.axis_size("tensor")
    seq_len = groups * row_count
    heads_here = rel_bias.shape[1]
    bucket_count = rel_bias.shape[0]
    local_width = w_query.shape[1]
    wide = -(-(local_width + 4) // 128) * 128
    gain_one, gain_two = norm1_gain.reshape(1, -1), norm2_gain.reshape(1, -1)
    router_t = w_router.T
    position = expert_route * c_send + slot_index
    position_row, position_col = position.reshape(1, -1), position.reshape(-1, 1)

    def dispatch(rows):
        return exchange(rows.reshape(experts, c_send, -1)).reshape(slots, -1)

    line_len = 2 * row_count + 2 * near_reach
    line_offsets = np.arange(line_len) - (row_count + near_reach)
    line_buckets = bucket_of(line_offsets, bucket_count)
    lookup = jnp.asarray(
        (line_buckets[:, None] == np.arange(bucket_count)[None, :]).astype(np.float32)
    )
    line = jnp.einsum("rb,bh->hr", lookup, rel_bias, precision=highest)
    wq_t, wk_t, wv_t = w_query.T, w_key.T, w_value.T
    pad = ((0, wide - local_width), (0, 0))
    wq_wide, wk_wide = jnp.pad(wq_t, pad), jnp.pad(wk_t, pad)
    segment_col = segment_ids.reshape(-1, 1)
    up_local, down_local = w_up[0], w_down[0]
    early = down_local.shape[0] * 5 // 16
    down_first, down_rest = down_local[:early], down_local[early:]

    hidden_across = swap(hidden_in, "tensor", 2)
    hidden_beside = swap(hidden_in, "tensor", 1)
    (
        hidden_across,
        line,
        wq_wide,
        wk_wide,
        segment_col,
        w_out_here,
        down_first,
        down_rest,
        position_row,
        position_col,
    ) = tie(
        hidden_across,
        line,
        wq_wide,
        wk_wide,
        segment_col,
        w_out,
        down_first,
        down_rest,
        position_row,
        position_col,
    )
    hidden_four = [hidden_in, hidden_beside, hidden_across, swap(hidden_across, "tensor", 1)]
    w_out_across = swap(w_out_here, "tensor", 2)
    w_out_beside = swap(w_out_here, "tensor", 1)
    down_early = swap(down_first, "tensor", 2)
    attention_flops = seq_len * seq_len * wide * heads_here * 14
    slab = ((heads_here, 2 * seq_len - row_count, row_count), full)
    normed_four, queries, keys_all, values_all, totals, *attended_four = run_local(
        functools.partial(forward_kernel, heads_here, groups),
        "attention_forward",
        [
            ((groups, row_count, model_width), low),
            ((seq_len, wide), low),
            ((seq_len, wide), low),
            ((seq_len, local_width), low),
            ((heads_here, seq_len), full),
        ]
        + [((row_count, local_width), low)] * groups,
        [slab, ((local_width, seq_len), low), ((groups, row_count, local_width), low)],
        attention_flops,
        me,
        *hidden_four,
        gain_one,
        wq_wide,
        wk_wide,
        wv_t,
        line,
        segment_col,
        scalar_first=True,
    )
    *attended_four, w_out_across, w_out_beside, down_early = tie(
        *attended_four, w_out_across, w_out_beside, down_early
    )
    w_out_four = [w_out_here, w_out_beside, w_out_across, swap(w_out_across, "tensor", 1)]
    attended_here = exchange_four(attended_four)
    *attended_here, up_first, down_rest = tie(*attended_here, up_local, down_rest)
    up_far = swap(up_first, "tensor", 2)
    down_late = swap(down_rest, "tensor", 2)
    middle, normed_two, send_rows = run_local(
        functools.partial(output_kernel, groups),
        "output_projection",
        [
            ((row_count, model_width), full),
            ((row_count, model_width), low),
            ((slots, 2 * model_width), low),
        ],
        [],
        0,
        *attended_here,
        *w_out_four,
        hidden_in,
        gain_two,
        position_row,
        out_grad,
    )
    rows_here = dispatch(send_rows)
    rows_here, up_far = tie(rows_here, up_far)
    rows_beside = swap(rows_here, "tensor", 1)

    both, hidden_here = 2 * slots, up_local.shape[1]
    expert_flops = 0
    produced_near, rows_near, active_near, pre_grad_near, gated, probs = run_local(
        near_kernel,
        "expert_near",
        [
            ((both, model_width), low),
            ((both, model_width), low),
            ((both, hidden_here), low),
            ((both, hidden_here), low),
            ((both, model_width), low),
            ((slots, experts), full),
        ],
        [],
        expert_flops,
        expert_me,
        rows_here,
        rows_beside,
        router_t,
        up_local,
        down_local,
        scalar_first=True,
    )
    rows_near, down_late = tie(rows_near, down_late)
    produced_own, produced_other, rows_own, rows_other, active_far, pre_grad_far = run_local(
        far_kernel,
        "expert_far",
        [
            ((slots, model_width), low),
            ((slots, model_width), low),
            ((slots, model_width), low),
            ((slots, model_width), low),
            ((both, hidden_here), low),
            ((both, hidden_here), low),
        ],
        [],
        expert_flops,
        rows_here,
        rows_beside,
        gated,
        up_far,
        down_early,
        down_late,
        produced_near,
        rows_near,
    )
    produced, rows_back, router_grad = run_local(
        finish_kernel,
        "expert_finish",
        [
            ((slots, model_width), low),
            ((slots, model_width), low),
            ((experts, model_width), full),
        ],
        [],
        0,
        expert_me,
        produced_own,
        swap(produced_other, "tensor", 1),
        rows_own,
        swap(rows_other, "tensor", 1),
        rows_here,
        probs,
        router_t,
        scalar_first=True,
    )

    grads_back = dispatch(rows_back)

    def of_weights(left, right):
        return jnp.einsum("cd,cf->df", left, right, preferred_element_type=full)

    expert_rows = jnp.concatenate([rows_here[:, :model_width], rows_beside[:, :model_width]])
    down_sent = of_weights(active_far, gated).astype(low)
    half = down_sent.shape[0] // 2
    grads_back, produced, down_one, down_two, up_sent, up_near, down_near = tie(
        grads_back,
        produced,
        down_sent[:half],
        down_sent[half:],
        of_weights(expert_rows, pre_grad_far).astype(low),
        of_weights(expert_rows, pre_grad_near),
        of_weights(active_near, gated),
    )
    middle_grad, gain_two_grad, out_own, out_beside, out_across, out_corner, *grad_four = run_local(
        functools.partial(token_kernel, groups),
        "token_backward",
        [
            ((row_count, model_width), full),
            ((1, model_width), full),
            ((local_width, model_width), low),
            ((local_width, model_width), low),
            ((local_width, model_width), low),
            ((local_width, model_width), low),
        ]
        + [((row_count, local_width), low)] * groups,
        [],
        0,
        grads_back,
        position_col,
        middle,
        gain_two,
        out_grad,
        *w_out_four,
        *attended_here,
    )
    grad_four = exchange_four(grad_four)
    out_came = swap(out_beside, "tensor", 1).astype(full)
    out_sent = (out_across.astype(full) + swap(out_corner, "tensor", 1).astype(full)).astype(low)
    *grad_four, out_sent, down_one = tie(*grad_four, out_sent, down_one)
    out_last = swap(out_sent, "tensor", 2)
    down_one = swap(down_one, "tensor", 2)
    grad_four[1], produced = tie(grad_four[1], produced)
    returned = dispatch(produced)

    backward = run_local(
        functools.partial(backward_kernel, heads_here, groups),
        "attention_backward",
        [
            ((3 * local_width, model_width), low),
            ((row_count, model_width), low),
            ((row_count, model_width), low),
            ((row_count, model_width), low),
            ((row_count, model_width), low),
            ((1, model_width), full),
            ((heads_here, line_len), full),
            ((2 * heads_here, row_count), full),
        ],
        [
            slab,
            slab,
            ((wide, seq_len), low),
            ((wide, seq_len), low),
            ((seq_len, local_width), low),
            ((local_width, seq_len), low),
            ((heads_here, seq_len), full),
            ((seq_len, seq_len), low),
            ((seq_len, seq_len), low),
            ((3 * local_width, seq_len), low),
        ],
        0,
        me,
        queries,
        keys_all,
        values_all,
        totals,
        line,
        wq_t,
        wk_t,
        wv_t,
        normed_four,
        gain_one,
        *grad_four,
        *attended_four,
        scalar_first=True,
    )
    (
        weight_grad,
        own_part,
        beside_part,
        across_part,
        corner_part,
        gain_one_grad,
        near_grad,
        far_grad,
    ) = backward
    corner_came = swap(corner_part, "tensor", 1).astype(full)
    beside_came = swap(beside_part, "tensor", 1).astype(full)
    across_sent = (across_part.astype(full) + corner_came).astype(low)
    up_one = swap(up_sent[: up_sent.shape[0] // 2], "tensor", 2)
    out_weight_grad = (out_own.astype(full) + out_came + out_last.astype(full)).astype(low)
    dense_rows = 4 * local_width
    count = lax.axis_size("dp")
    dense = jnp.concatenate([weight_grad, out_weight_grad]).reshape(count, -1, model_width)
    dense, returned, down_one = tie(dense, returned, down_one)
    dense = jnp.sum(exchange(dense).astype(full), axis=0).astype(low)

    far_here = jnp.sum(far_grad, axis=1).reshape(2, heads_here)
    rel_grad = jnp.einsum("rb,hr->hb", lookup, near_grad, precision=highest)
    far_place = np.zeros((2, bucket_count), np.float32)
    far_place[0, bucket_count // 2 - 1] = 1.0
    far_place[1, bucket_count - 1] = 1.0
    rel_grad = rel_grad + jnp.sum(far_here[:, :, None] * far_place[:, None, :], axis=0)
    rel_place = (jnp.arange(groups, dtype=jnp.int32) == tensor_me).astype(full)
    rel_wide = rel_place[:, None, None] * rel_grad[None]
    flat = jnp.concatenate(
        [
            gain_one_grad.reshape(-1),
            gain_two_grad.reshape(-1),
            router_grad.reshape(-1),
            rel_wide.reshape(-1),
        ]
    )
    flat_rows = -(-flat.shape[0] // (16 * model_width)) * 16
    flat = flat + swap(flat, "tensor", 2)
    flat = flat + swap(flat, "tensor", 1)
    flat = jnp.pad(flat, (0, flat_rows * model_width - flat.shape[0]))
    payload = jnp.concatenate([dense, flat.reshape(flat_rows, model_width).astype(low)])
    across = swap(across_sent, "tensor", 2)
    rest = jnp.concatenate([up_sent[up_sent.shape[0] // 2 :], down_two])
    payload, returned, up_one, across, rest = tie(payload, returned, up_one, across, rest)
    rest = swap(rest, "tensor", 2)
    payload = exchange(jnp.broadcast_to(payload[None], (count, *payload.shape)))
    dense, flat = payload[:, : dense_rows // count], payload[:, dense_rows // count :]
    dense = dense.reshape(dense_rows, model_width)

    normed_grad = rounded(own_part.astype(full) + beside_came + across.astype(full))
    inputs_f = hidden_in.astype(full)
    unused, scale_one = rms_forward(inputs_f, norm1_gain)
    input_part, unused = rms_backward(inputs_f, scale_one, norm1_gain, normed_grad)
    input_grad = middle_grad + input_part
    (layer_out,) = run_local(
        layer_kernel,
        "layer_output",
        [((row_count, model_width), low)],
        [],
        12 * 10**9,
        returned,
        position_col,
        expert_route.reshape(-1, 1),
        middle,
        normed_two,
        router_t,
    )
    layer_out, rest = tie(layer_out, rest)
    up_grad = up_near + jnp.concatenate([up_one, rest[:half]]).astype(full)
    down_grad = down_near + jnp.concatenate([down_one, rest[half:]]).astype(full)
    dense = dense.astype(full)
    flat = jnp.sum(flat.astype(full), axis=0).reshape(-1)
    gain_one_grad = flat[:model_width]
    gain_two_grad = flat[model_width : 2 * model_width]
    split = 2 * model_width + model_width * experts
    router_grad = flat[2 * model_width : split].reshape(experts, model_width).T
    rel_all = flat[split : split + groups * heads_here * bucket_count]
    rel_grad = pick(rel_all.reshape(groups, heads_here, bucket_count), tensor_me).T
    return (
        layer_out,
        input_grad,
        gain_one_grad,
        dense[:local_width].T,
        dense[local_width : 2 * local_width].T,
        dense[2 * local_width : 3 * local_width].T,
        dense[3 * local_width :],
        rel_grad,
        gain_two_grad,
        router_grad,
        up_grad[None],
        down_grad[None],
    )


def solution(mesh):
    return jax.shard_map(
        per_device,
        mesh=mesh,
        in_specs=(
            P(("dp", "tensor"), None),
            P("dp", None),
            P(("dp", "tensor")),
            P(("dp", "tensor")),
            P(),
            P(None, "tensor"),
            P(None, "tensor"),
            P(None, "tensor"),
            P("tensor", None),
            P(None, "tensor"),
            P(),
            P(),
            P("dp", None, "tensor"),
            P("dp", "tensor", None),
            P(("dp", "tensor"), None),
        ),
        out_specs=(
            P(("dp", "tensor"), None),
            P(("dp", "tensor"), None),
            P(),
            P(None, "tensor"),
            P(None, "tensor"),
            P(None, "tensor"),
            P("tensor", None),
            P(None, "tensor"),
            P(),
            P(),
            P("dp", None, "tensor"),
            P("dp", "tensor", None),
        ),
        check_vma=False,
    )
```

```python
import functools

import jax
import jax.numpy as jnp
import numpy as np
from jax import lax
from jax.experimental import pallas as pl
from jax.experimental.pallas import tpu as pltpu
from jax.sharding import PartitionSpec as P

highest = lax.Precision.HIGHEST
epsilon = 1e-06
apart = 2.0**30
near_reach = 128


def bucket_of(offsets, bucket_count):
    half_count = bucket_count // 2
    exact_count = half_count // 2
    upward = (offsets > 0).astype(np.int32) * half_count
    distance = np.abs(offsets)
    scaled = (
        np.log(np.maximum(distance, 1) / exact_count)
        / np.log(128 / exact_count)
        * (half_count - exact_count)
    )
    distant = np.minimum(exact_count + np.floor(scaled).astype(np.int32), half_count - 1)
    return (upward + np.where(distance < exact_count, distance, distant)).astype(np.int32)


def rounded(values):
    return lax.optimization_barrier(values.astype(jnp.bfloat16)).astype(jnp.float32)


def rms_forward(values, gain_vec):
    scale_row = lax.rsqrt(jnp.mean(values * values, axis=-1, keepdims=True) + epsilon)
    return (values * scale_row * gain_vec, scale_row)


def rms_backward(values, scale_row, gain_vec, normed_grad):
    gain_grad = jnp.sum(normed_grad * values * scale_row, axis=0)
    grad_hat = normed_grad * gain_vec
    row_inner = jnp.mean(grad_hat * values, axis=-1, keepdims=True)
    return (scale_row * (grad_hat - values * scale_row * scale_row * row_inner), gain_grad)


def swap(values, axis_name, bits):
    count = lax.axis_size(axis_name)
    return lax.ppermute(values, axis_name, [(i, i ^ bits) for i in range(count)])


def power_of_two(axis_name):
    count = lax.axis_size(axis_name)
    return count <= 8 and count & (count - 1) == 0


def exchange(chunks):
    return lax.all_to_all(chunks, "dp", split_axis=0, concat_axis=0, tiled=True)


def exchange_four(chunks):
    parts = [swap(chunks[k], "tensor", k) for k in range(1, lax.axis_size("tensor"))]
    return [chunks[0]] + parts


def gather_four(values):
    across = swap(values, "tensor", 2)
    beside = swap(values, "tensor", 1)
    return [values, beside, across, swap(across, "tensor", 1)]


def tie(*arrays):
    return lax.optimization_barrier(arrays)


def pick(stacked, index):
    return lax.dynamic_index_in_dim(stacked, index, axis=0, keepdims=False)


gelu_c = float(np.sqrt(2.0 / np.pi))


def gelu_and_slope(values):
    square = values * values
    bent = jnp.tanh(gelu_c * values * (1.0 + 0.044715 * square))
    half = 0.5 * (1.0 + bent)
    slope = half + 0.5 * values * (1.0 - bent * bent) * (
        gelu_c * (1.0 + 3 * 0.044715 * square)
    )
    return values * half, slope


def dot_nt(left, right):
    return lax.dot_general(
        left, right, (((1,), (1,)), ((), ())), preferred_element_type=jnp.float32
    )


def dot_nn(left, right):
    return lax.dot_general(
        left, right, (((1,), (0,)), ((), ())), preferred_element_type=jnp.float32
    )


def fill_slab(line_ref, slab_ref, heads, block):
    slab_rows = slab_ref.shape[1]
    near_rows = block + 2 * near_reach
    near_start = (slab_rows - near_rows + block) // 2 - block // 2
    line_len = line_ref.shape[1]
    for h in range(heads):
        line = line_ref[h : h + 1, :]
        rolled = pltpu.roll(
            jnp.broadcast_to(line, (block, line_len)), 0, axis=1, stride=1, stride_axis=0
        )
        slab_ref[h, near_start : near_start + near_rows, :] = rolled[:, block:].T
        slab_ref[h, :near_start, :] = jnp.broadcast_to(line[:, :1], (near_start, block))
        after = near_start + near_rows
        slab_ref[h, after:, :] = jnp.broadcast_to(
            line[:, line_len - 1 :], (slab_rows - after, block)
        )


def key_spans(groups):
    if groups != 4:
        return [(list(range(groups)), groups)]
    return [([1, 2], 4), ([0, 3], 3)]


def over_blocks(groups, block, one_block, unroll):
    for blocks, key_blocks in key_spans(groups):
        low, step = blocks[0], blocks[1] - blocks[0]

        def body(j, carry, low=low, step=step, key_blocks=key_blocks):
            i = low + step * j
            one_block(i, j if key_blocks < groups else 0, key_blocks * block)
            return carry

        lax.fori_loop(0, len(blocks), body, 0, unroll=unroll)


def forward_kernel(
    heads,
    groups,
    me_ref,
    *refs,
):
    parts = refs[:groups]
    (
        gain_ref,
        wq_ref,
        wk_ref,
        wv_ref,
        line_ref,
        segment_ref,
        normed_ref,
        q_ref,
        k_ref,
        v_ref,
        total_ref,
    ) = refs[groups : groups + 11]
    outputs_to = refs[groups + 11 : 2 * groups + 11]
    slab_ref, vt_ref, attended_ref = refs[2 * groups + 11 :]
    me = me_ref[0]
    block = parts[0].shape[0]
    local_width = v_ref.shape[1]
    wide = q_ref.shape[1]
    head_size = local_width // heads
    seq_len = groups * block
    fill_slab(line_ref, slab_ref, heads, block)
    lane = lax.broadcasted_iota(jnp.int32, (block, wide), 1)
    for k in range(groups):
        here = pl.ds(pl.multiple_of((k ^ me) * block, block), block)
        part, unused = rms_forward(parts[k][...].astype(jnp.float32), gain_ref[...])
        part = part.astype(jnp.bfloat16)
        normed_ref[k] = part
        mark = lane - local_width == segment_ref[here, :]
        queries = dot_nt(part, wq_ref[...]).astype(jnp.bfloat16).astype(jnp.float32)
        queries = queries * head_size ** (-0.5)
        q_ref[here, :] = jnp.where(mark, -apart, queries).astype(jnp.bfloat16)
        keys = dot_nt(part, wk_ref[...])
        other = jnp.logical_and(lane >= local_width, jnp.logical_not(mark))
        k_ref[here, :] = jnp.where(other, 1.0, keys).astype(jnp.bfloat16)
        values = dot_nt(part, wv_ref[...])
        v_ref[here, :] = values.astype(jnp.bfloat16)
        vt_ref[:, here] = values.T.astype(jnp.bfloat16)
    block_lane = lax.broadcasted_iota(jnp.int32, (block, wide), 1)

    def one_block(i, first, key_count):
        here = pl.ds(pl.multiple_of(i * block, block), block)
        keys = pl.ds(pl.multiple_of(first * block, block), key_count)
        places = pl.ds(pl.multiple_of((groups - 1 - i + first) * block, block), key_count)
        query_blk = q_ref[here, :]
        outputs = []
        for h in range(heads):
            mine = jnp.logical_or(
                jnp.logical_and(block_lane >= h * head_size, block_lane < (h + 1) * head_size),
                block_lane >= local_width,
            )
            query = jnp.where(mine, query_blk, jnp.zeros_like(query_blk))
            scores = dot_nt(k_ref[keys, :], query) + slab_ref[h, places, :]
            peak = jnp.max(scores, axis=0, keepdims=True)
            weights = jnp.exp(scores - peak)
            total = jnp.sum(weights, axis=0, keepdims=True)
            out = dot_nn(
                vt_ref[h * head_size : (h + 1) * head_size, keys], weights.astype(jnp.bfloat16)
            )
            outputs.append(out * (1.0 / total))
            total_ref[h : h + 1, here] = peak + jnp.log(total)
        outputs = jnp.concatenate(outputs, axis=0)
        attended_ref[i ^ me] = outputs.T.astype(jnp.bfloat16)

    over_blocks(groups, block, one_block, False)
    for k, output in enumerate(outputs_to):
        output[...] = attended_ref[k]


def backward_kernel(
    heads,
    groups,
    me_ref,
    q_ref,
    k_ref,
    v_ref,
    total_ref,
    line_ref,
    wq_ref,
    wk_ref,
    wv_ref,
    normed_ref,
    gain_ref,
    *refs,
):
    grads_in, attended_in = refs[:groups], refs[groups : 2 * groups]
    (
        weight_ref,
        *model_refs,
        gain_grad_ref,
        near_ref,
        far_ref,
        slab_ref,
        diag_ref,
        kt_ref,
        qt_ref,
        out_ref,
        out_t_ref,
        inner_ref,
        p_ref,
        ds_ref,
        grad_t_ref,
    ) = refs[2 * groups :]
    me = me_ref[0]
    seq_len, local_width = v_ref.shape
    wide = q_ref.shape[1]
    head_size = local_width // heads
    block = seq_len // groups
    fill_slab(line_ref, slab_ref, heads, block)
    diag_ref[...] = jnp.zeros_like(diag_ref)
    for k in range(groups):
        here = pl.ds(pl.multiple_of((k ^ me) * block, block), block)
        grads = grads_in[k][...]
        out_ref[here, :] = grads
        grads = grads.astype(jnp.float32)
        out_t_ref[:, here] = grads.T.astype(jnp.bfloat16)
        products = (grads * attended_in[k][...].astype(jnp.float32)).T
        for h in range(heads):
            inner_ref[h : h + 1, here] = jnp.sum(
                products[h * head_size : (h + 1) * head_size], axis=0, keepdims=True
            )
        kt_ref[:, here] = k_ref[here, :].astype(jnp.float32).T.astype(jnp.bfloat16)
        qt_ref[:, here] = q_ref[here, :].astype(jnp.float32).T.astype(jnp.bfloat16)
    wide_lane = lax.broadcasted_iota(jnp.int32, (block, wide), 1)
    lane = lax.broadcasted_iota(jnp.int32, (block, local_width), 1)
    for h in range(heads):
        low, high = h * head_size, (h + 1) * head_size
        mine = jnp.logical_or(
            jnp.logical_and(wide_lane >= low, wide_lane < high), wide_lane >= local_width
        )
        head_lanes = jnp.logical_and(lane >= low, lane < high)

        def one_block(i, first, key_count, low=low, high=high, mine=mine, head_lanes=head_lanes):
            here = pl.ds(pl.multiple_of(i * block, block), block)
            keys = pl.ds(pl.multiple_of(first * block, block), key_count)
            places = pl.ds(pl.multiple_of((groups - 1 - i + first) * block, block), key_count)
            query_blk = q_ref[here, :]
            query = jnp.where(mine, query_blk, jnp.zeros_like(query_blk))
            grad_blk = out_ref[here, :]
            grad = jnp.where(head_lanes, grad_blk, jnp.zeros_like(grad_blk))
            scores = dot_nt(k_ref[keys, :], query) + slab_ref[h, places, :]
            probs = jnp.exp(scores - total_ref[h : h + 1, here])
            prob_grad = dot_nt(v_ref[keys, :], grad)
            score_grad = probs * (prob_grad - inner_ref[h : h + 1, here])
            score_low = score_grad.astype(jnp.bfloat16)
            p_ref[keys, here] = probs.astype(jnp.bfloat16)
            ds_ref[keys, here] = score_low
            diag_ref[h, places, :] += score_grad
            query_grad = dot_nn(kt_ref[low:high, keys], score_low) * head_size ** (-0.5)
            grad_t_ref[low:high, here] = query_grad.astype(jnp.bfloat16)

        over_blocks(groups, block, one_block, True)
        for j in range(groups):
            keys = slice(j * block, (j + 1) * block)
            first, last = (max(0, j - 2), min(groups, j + 3)) if groups == 4 else (0, groups)
            meet = slice(first * block, last * block)
            grad_t_ref[local_width + low : local_width + high, keys] = dot_nt(
                qt_ref[low:high, meet], ds_ref[keys, meet]
            ).astype(jnp.bfloat16)
            grad_t_ref[2 * local_width + low : 2 * local_width + high, keys] = dot_nt(
                out_t_ref[low:high, meet], p_ref[keys, meet]
            ).astype(jnp.bfloat16)
    weight_grad = jnp.zeros(weight_ref.shape, jnp.float32)
    gain_grad = jnp.zeros(gain_grad_ref.shape, jnp.float32)
    for k in range(groups):
        here = pl.ds(pl.multiple_of((k ^ me) * block, block), block)
        blk = grad_t_ref[:, here]
        weight_grad += dot_nn(blk, normed_ref[k])
        model = jnp.zeros(model_refs[0].shape, jnp.float32)
        for part, w_ref in enumerate((wq_ref, wk_ref, wv_ref)):
            piece = blk[part * local_width : (part + 1) * local_width, :]
            model += dot_nn(piece.astype(jnp.float32).T.astype(jnp.bfloat16), w_ref[...])
        model_refs[k][...] = model.astype(jnp.bfloat16)
        gain_grad += jnp.sum(model * normed_ref[k].astype(jnp.float32), axis=0, keepdims=True)
    gain_grad_ref[...] = gain_grad / gain_ref[...]
    weight_ref[...] = weight_grad.astype(jnp.bfloat16)
    slab_rows = diag_ref.shape[1]
    near_rows = block + 2 * near_reach
    near_start = (slab_rows - near_rows) // 2
    line_len = line_ref.shape[1]
    row_id = lax.broadcasted_iota(jnp.int32, (block, line_len), 0)
    for h in range(heads):
        near = diag_ref[h, near_start : near_start + near_rows, :].T
        near = jnp.concatenate([jnp.zeros((block, line_len - near_rows), jnp.float32), near], axis=1)
        bit = 1
        while bit < block:
            near = jnp.where(
                (row_id // bit) % 2 == 1, pltpu.roll(near, line_len - bit, axis=1), near
            )
            bit *= 2
        near_ref[h : h + 1, :] = jnp.sum(near, axis=0, keepdims=True)
        far_ref[h : h + 1, :] = jnp.sum(diag_ref[h, :near_start, :], axis=0, keepdims=True)
        far_ref[heads + h : heads + h + 1, :] = jnp.sum(
            diag_ref[h, near_start + near_rows :, :], axis=0, keepdims=True
        )


def output_kernel(groups, *refs):
    attended, weights = refs[:groups], refs[groups : 2 * groups]
    hidden_ref, gain_ref, position_ref, grad_ref, middle_ref, normed_ref, send_ref = refs[
        2 * groups :
    ]
    middle = hidden_ref[...].astype(jnp.float32)
    for part, weight in zip(attended, weights):
        middle += dot_nn(part[...], weight[...])
    middle_ref[...] = middle
    normed, unused = rms_forward(middle, gain_ref[...])
    normed = normed.astype(jnp.bfloat16)
    normed_ref[...] = normed
    shape = (send_ref.shape[0], middle.shape[0])
    here = lax.broadcasted_iota(jnp.int32, shape, 0) == position_ref[...]
    here = here.astype(jnp.bfloat16)
    width = middle.shape[1]
    send_ref[:, :width] = dot_nn(here, normed).astype(jnp.bfloat16)
    send_ref[:, width:] = dot_nn(here, grad_ref[...]).astype(jnp.bfloat16)


def token_kernel(
    groups, back_ref, position_ref, middle_ref, gain_ref, grad_ref, *refs
):
    weights, attended = refs[:groups], refs[groups : 2 * groups]
    total_ref, gain_grad_ref, *blocks = refs[2 * groups : 3 * groups + 2]
    outputs = refs[3 * groups + 2 :]
    shape = (middle_ref.shape[0], back_ref.shape[0])
    here = lax.broadcasted_iota(jnp.int32, shape, 1) == position_ref[...]
    normed_grad = dot_nn(here.astype(jnp.bfloat16), back_ref[...])
    middle = middle_ref[...]
    scale = lax.rsqrt(jnp.mean(middle * middle, axis=-1, keepdims=True) + epsilon)
    gain_grad_ref[...] = jnp.sum(normed_grad * middle * scale, axis=0, keepdims=True)
    hat = normed_grad * gain_ref[...]
    inner = jnp.mean(hat * middle, axis=-1, keepdims=True)
    total = grad_ref[...].astype(jnp.float32) + scale * (hat - middle * scale * scale * inner)
    total_ref[...] = total
    low = total.astype(jnp.bfloat16)
    for k, (weight, part, output) in enumerate(zip(weights, attended, outputs)):
        output[...] = dot_nt(low, weight[...]).astype(jnp.bfloat16)
        weight_grad = dot_nn(part[...].astype(jnp.float32).T.astype(jnp.bfloat16), low)
        blocks[k][...] = weight_grad.astype(blocks[k].dtype)


def router_of(rows, router):
    logits = lax.dot_general(
        rows.astype(jnp.float32),
        router,
        (((1,), (1,)), ((), ())),
        precision=highest,
        preferred_element_type=jnp.float32,
    )
    raised = jnp.exp(logits - jnp.max(logits, axis=-1, keepdims=True))
    return raised / jnp.sum(raised, axis=-1, keepdims=True)


def layer_kernel(
    returned_ref, position_ref, route_ref, middle_ref, normed_ref, router_ref, output_ref
):
    probs = router_of(normed_ref[...], router_ref[...])
    chosen = lax.broadcasted_iota(jnp.int32, probs.shape, 1) == route_ref[...]
    gate = jnp.sum(jnp.where(chosen, probs, 0.0), axis=-1, keepdims=True)
    shape = (middle_ref.shape[0], returned_ref.shape[0])
    here = lax.broadcasted_iota(jnp.int32, shape, 1) == position_ref[...]
    produced = dot_nn(here.astype(jnp.bfloat16), returned_ref[...])
    output_ref[...] = (middle_ref[...] + gate * produced).astype(jnp.bfloat16)


def near_kernel(
    me_ref,
    own_ref,
    beside_ref,
    router_ref,
    up_ref,
    down_ref,
    produced_ref,
    rows_ref,
    active_ref,
    pre_grad_ref,
    gated_ref,
    probs_ref,
):
    me = me_ref[0]
    slots = own_ref.shape[0]
    width = up_ref.shape[0]
    for k, both_ref in enumerate((own_ref, beside_ref)):
        here = slice(k * slots, (k + 1) * slots)
        rows = both_ref[:, :width]
        probs = router_of(rows, router_ref[...])
        if k == 0:
            probs_ref[...] = probs
        chosen = lax.broadcasted_iota(jnp.int32, probs.shape, 1) == me
        gate = jnp.sum(jnp.where(chosen, probs, 0.0), axis=-1, keepdims=True)
        gated = (gate * both_ref[:, width:].astype(jnp.float32)).astype(jnp.bfloat16)
        gated_ref[here, :] = gated
        active, slope = gelu_and_slope(dot_nn(rows, up_ref[...]))
        active = active.astype(jnp.bfloat16)
        active_ref[here, :] = active
        produced_ref[here, :] = dot_nn(active, down_ref[...]).astype(jnp.bfloat16)
        active_grad = dot_nt(gated, down_ref[...]).astype(jnp.bfloat16).astype(jnp.float32)
        pre_grad = (active_grad * slope).astype(jnp.bfloat16)
        pre_grad_ref[here, :] = pre_grad
        rows_ref[here, :] = dot_nt(pre_grad, up_ref[...]).astype(jnp.bfloat16)


def far_kernel(
    own_ref,
    beside_ref,
    gated_ref,
    up_ref,
    early_ref,
    late_ref,
    produced_in_ref,
    rows_in_ref,
    produced_ref,
    produced_other_ref,
    rows_ref,
    rows_other_ref,
    active_ref,
    pre_grad_ref,
):
    slots = own_ref.shape[0]
    cut = early_ref.shape[0]
    for k, row_ref in enumerate((own_ref, beside_ref)):
        here = slice(k * slots, (k + 1) * slots)
        active, slope = gelu_and_slope(dot_nn(row_ref[:, : up_ref.shape[0]], up_ref[...]))
        active = active.astype(jnp.bfloat16)
        active_ref[here, :] = active
        produced = produced_in_ref[here, :].astype(jnp.float32) + dot_nn(active[:, :cut], early_ref[...])
        produced = produced + dot_nn(active[:, cut:], late_ref[...])
        gated = gated_ref[here, :]
        active_grad = jnp.concatenate(
            [dot_nt(gated, early_ref[...]), dot_nt(gated, late_ref[...])], axis=1
        )
        active_grad = active_grad.astype(jnp.bfloat16).astype(jnp.float32)
        pre_grad = (active_grad * slope).astype(jnp.bfloat16)
        pre_grad_ref[here, :] = pre_grad
        back = rows_in_ref[here, :].astype(jnp.float32) + dot_nt(pre_grad, up_ref[...])
        if k == 0:
            produced_ref[...] = produced.astype(jnp.bfloat16)
            rows_ref[...] = back.astype(jnp.bfloat16)
        else:
            produced_other_ref[...] = produced.astype(jnp.bfloat16)
            rows_other_ref[...] = back.astype(jnp.bfloat16)


def finish_kernel(
    me_ref,
    produced_in_ref,
    produced_came_ref,
    rows_in_ref,
    rows_came_ref,
    own_ref,
    probs_ref,
    router_ref,
    produced_ref,
    back_ref,
    router_grad_ref,
):
    me = me_ref[0]
    produced = produced_in_ref[...].astype(jnp.float32) + produced_came_ref[...].astype(jnp.float32)
    produced = produced.astype(jnp.bfloat16)
    produced_ref[...] = produced
    width = produced.shape[1]
    gate_grad = jnp.sum(
        own_ref[:, width:].astype(jnp.float32) * produced.astype(jnp.float32), axis=-1, keepdims=True
    )
    probs = probs_ref[...]
    chosen = (lax.broadcasted_iota(jnp.int32, probs.shape, 1) == me).astype(jnp.float32)
    gate = jnp.sum(chosen * probs, axis=-1, keepdims=True)
    logit_grad = probs * (chosen - gate) * gate_grad
    back = rows_in_ref[...].astype(jnp.float32) + rows_came_ref[...].astype(jnp.float32)
    back = back.astype(jnp.bfloat16).astype(jnp.float32)
    term = lax.dot_general(
        logit_grad,
        router_ref[...],
        (((1,), (0,)), ((), ())),
        precision=highest,
        preferred_element_type=jnp.float32,
    )
    back_ref[...] = (back + term).astype(jnp.bfloat16)
    router_grad_ref[...] = lax.dot_general(
        logit_grad.T,
        own_ref[:, :width].astype(jnp.float32),
        (((1,), (0,)), ((), ())),
        precision=highest,
        preferred_element_type=jnp.float32,
    )


def run_local(kernel, name, outs, scratch, flops, *arrays, scalar_first=False):
    in_specs = [pl.BlockSpec(memory_space=pltpu.VMEM)] * len(arrays)
    if scalar_first:
        in_specs[0] = pl.BlockSpec(memory_space=pltpu.SMEM)
    return pl.pallas_call(
        kernel,
        out_shape=tuple(jax.ShapeDtypeStruct(shape, kind) for shape, kind in outs),
        in_specs=in_specs,
        out_specs=tuple([pl.BlockSpec(memory_space=pltpu.VMEM)] * len(outs)),
        scratch_shapes=[pltpu.VMEM(shape, kind) for shape, kind in scratch],
        compiler_params=pltpu.CompilerParams(vmem_limit_bytes=60 * 1024 * 1024),
        cost_estimate=pl.CostEstimate(flops=flops, bytes_accessed=0, transcendentals=0),
        name=name,
    )(*arrays)


def per_device(
    hidden_in,
    segment_ids,
    expert_route,
    slot_index,
    norm1_gain,
    w_query,
    w_key,
    w_value,
    w_out,
    rel_bias,
    norm2_gain,
    w_router,
    w_up,
    w_down,
    out_grad,
):
    low, full = jnp.bfloat16, jnp.float32
    row_count, model_width = hidden_in.shape
    experts = w_router.shape[1]
    c_send = 3 * row_count // (2 * experts)
    slots = experts * c_send
    tensor_me = lax.axis_index("tensor").astype(jnp.int32)
    dp_me = lax.axis_index("dp").astype(jnp.int32)
    me, expert_me = tensor_me.reshape(1), dp_me.reshape(1)
    groups = lax.axis_size("tensor")
    seq_len = groups * row_count
    heads_here = rel_bias.shape[1]
    bucket_count = rel_bias.shape[0]
    local_width = w_query.shape[1]
    wide = -(-(local_width + 4) // 128) * 128
    gain_one, gain_two = norm1_gain.reshape(1, -1), norm2_gain.reshape(1, -1)
    router_t = w_router.T
    position = expert_route * c_send + slot_index
    position_row, position_col = position.reshape(1, -1), position.reshape(-1, 1)

    def dispatch(rows):
        return exchange(rows.reshape(experts, c_send, -1)).reshape(slots, -1)

    line_len = 2 * row_count + 2 * near_reach
    line_offsets = np.arange(line_len) - (row_count + near_reach)
    line_buckets = bucket_of(line_offsets, bucket_count)
    lookup = jnp.asarray(
        (line_buckets[:, None] == np.arange(bucket_count)[None, :]).astype(np.float32)
    )
    line = jnp.einsum("rb,bh->hr", lookup, rel_bias, precision=highest)
    wq_t, wk_t, wv_t = w_query.T, w_key.T, w_value.T
    pad = ((0, wide - local_width), (0, 0))
    wq_wide, wk_wide = jnp.pad(wq_t, pad), jnp.pad(wk_t, pad)
    segment_col = segment_ids.reshape(-1, 1)
    up_local, down_local = w_up[0], w_down[0]
    early = down_local.shape[0] * 5 // 16
    down_first, down_rest = down_local[:early], down_local[early:]

    hidden_across = swap(hidden_in, "tensor", 2)
    hidden_beside = swap(hidden_in, "tensor", 1)
    (
        hidden_across,
        line,
        wq_wide,
        wk_wide,
        segment_col,
        w_out_here,
        down_first,
        down_rest,
        position_row,
        position_col,
    ) = tie(
        hidden_across,
        line,
        wq_wide,
        wk_wide,
        segment_col,
        w_out,
        down_first,
        down_rest,
        position_row,
        position_col,
    )
    hidden_four = [hidden_in, hidden_beside, hidden_across, swap(hidden_across, "tensor", 1)]
    w_out_across = swap(w_out_here, "tensor", 2)
    w_out_beside = swap(w_out_here, "tensor", 1)
    down_early = swap(down_first, "tensor", 2)
    attention_flops = seq_len * seq_len * wide * heads_here * 14
    slab = ((heads_here, 2 * seq_len - row_count, row_count), full)
    normed_four, queries, keys_all, values_all, totals, *attended_four = run_local(
        functools.partial(forward_kernel, heads_here, groups),
        "attention_forward",
        [
            ((groups, row_count, model_width), low),
            ((seq_len, wide), low),
            ((seq_len, wide), low),
            ((seq_len, local_width), low),
            ((heads_here, seq_len), full),
        ]
        + [((row_count, local_width), low)] * groups,
        [slab, ((local_width, seq_len), low), ((groups, row_count, local_width), low)],
        attention_flops,
        me,
        *hidden_four,
        gain_one,
        wq_wide,
        wk_wide,
        wv_t,
        line,
        segment_col,
        scalar_first=True,
    )
    *attended_four, w_out_across, w_out_beside, down_early = tie(
        *attended_four, w_out_across, w_out_beside, down_early
    )
    w_out_four = [w_out_here, w_out_beside, w_out_across, swap(w_out_across, "tensor", 1)]
    attended_here = exchange_four(attended_four)
    *attended_here, up_first, down_rest = tie(*attended_here, up_local, down_rest)
    up_far = swap(up_first, "tensor", 2)
    down_late = swap(down_rest, "tensor", 2)
    middle, normed_two, send_rows = run_local(
        functools.partial(output_kernel, groups),
        "output_projection",
        [
            ((row_count, model_width), full),
            ((row_count, model_width), low),
            ((slots, 2 * model_width), low),
        ],
        [],
        0,
        *attended_here,
        *w_out_four,
        hidden_in,
        gain_two,
        position_row,
        out_grad,
    )
    rows_here = dispatch(send_rows)
    rows_here, up_far = tie(rows_here, up_far)
    rows_beside = swap(rows_here, "tensor", 1)

    both, hidden_here = 2 * slots, up_local.shape[1]
    expert_flops = 0
    produced_near, rows_near, active_near, pre_grad_near, gated, probs = run_local(
        near_kernel,
        "expert_near",
        [
            ((both, model_width), low),
            ((both, model_width), low),
            ((both, hidden_here), low),
            ((both, hidden_here), low),
            ((both, model_width), low),
            ((slots, experts), full),
        ],
        [],
        expert_flops,
        expert_me,
        rows_here,
        rows_beside,
        router_t,
        up_local,
        down_local,
        scalar_first=True,
    )
    rows_near, down_late = tie(rows_near, down_late)
    produced_own, produced_other, rows_own, rows_other, active_far, pre_grad_far = run_local(
        far_kernel,
        "expert_far",
        [
            ((slots, model_width), low),
            ((slots, model_width), low),
            ((slots, model_width), low),
            ((slots, model_width), low),
            ((both, hidden_here), low),
            ((both, hidden_here), low),
        ],
        [],
        expert_flops,
        rows_here,
        rows_beside,
        gated,
        up_far,
        down_early,
        down_late,
        produced_near,
        rows_near,
    )
    produced, rows_back, router_grad = run_local(
        finish_kernel,
        "expert_finish",
        [
            ((slots, model_width), low),
            ((slots, model_width), low),
            ((experts, model_width), full),
        ],
        [],
        0,
        expert_me,
        produced_own,
        swap(produced_other, "tensor", 1),
        rows_own,
        swap(rows_other, "tensor", 1),
        rows_here,
        probs,
        router_t,
        scalar_first=True,
    )

    grads_back = dispatch(rows_back)

    def of_weights(left, right):
        return jnp.einsum("cd,cf->df", left, right, preferred_element_type=full)

    expert_rows = jnp.concatenate([rows_here[:, :model_width], rows_beside[:, :model_width]])
    down_sent = of_weights(active_far, gated).astype(low)
    half, cut = up_local.shape[0] // 2, down_local.shape[0] * 5 // 12
    grads_back, produced, down_one, down_two, up_sent, up_near, down_near = tie(
        grads_back,
        produced,
        down_sent[:cut],
        down_sent[cut:],
        of_weights(expert_rows, pre_grad_far).astype(low),
        of_weights(expert_rows, pre_grad_near),
        of_weights(active_near, gated),
    )
    middle_grad, gain_two_grad, out_own, out_beside, out_across, out_corner, *grad_four = run_local(
        functools.partial(token_kernel, groups),
        "token_backward",
        [
            ((row_count, model_width), full),
            ((1, model_width), full),
            ((local_width, model_width), low),
            ((local_width, model_width), low),
            ((local_width, model_width), low),
            ((local_width, model_width), low),
        ]
        + [((row_count, local_width), low)] * groups,
        [],
        0,
        grads_back,
        position_col,
        middle,
        gain_two,
        out_grad,
        *w_out_four,
        *attended_here,
    )
    grad_four = exchange_four(grad_four)
    out_came = swap(out_beside, "tensor", 1).astype(full)
    out_sent = (out_across.astype(full) + swap(out_corner, "tensor", 1).astype(full)).astype(low)
    *grad_four, out_sent, down_one = tie(*grad_four, out_sent, down_one)
    out_last = swap(out_sent, "tensor", 2)
    down_one = swap(down_one, "tensor", 2)
    grad_four[1], produced = tie(grad_four[1], produced)
    returned = dispatch(produced)

    backward = run_local(
        functools.partial(backward_kernel, heads_here, groups),
        "attention_backward",
        [
            ((3 * local_width, model_width), low),
            ((row_count, model_width), low),
            ((row_count, model_width), low),
            ((row_count, model_width), low),
            ((row_count, model_width), low),
            ((1, model_width), full),
            ((heads_here, line_len), full),
            ((2 * heads_here, row_count), full),
        ],
        [
            slab,
            slab,
            ((wide, seq_len), low),
            ((wide, seq_len), low),
            ((seq_len, local_width), low),
            ((local_width, seq_len), low),
            ((heads_here, seq_len), full),
            ((seq_len, seq_len), low),
            ((seq_len, seq_len), low),
            ((3 * local_width, seq_len), low),
        ],
        0,
        me,
        queries,
        keys_all,
        values_all,
        totals,
        line,
        wq_t,
        wk_t,
        wv_t,
        normed_four,
        gain_one,
        *grad_four,
        *attended_four,
        scalar_first=True,
    )
    (
        weight_grad,
        own_part,
        beside_part,
        across_part,
        corner_part,
        gain_one_grad,
        near_grad,
        far_grad,
    ) = backward
    corner_came = swap(corner_part, "tensor", 1).astype(full)
    beside_came = swap(beside_part, "tensor", 1).astype(full)
    across_sent = (across_part.astype(full) + corner_came).astype(low)
    up_one = swap(up_sent[:half], "tensor", 2)
    out_weight_grad = (out_own.astype(full) + out_came + out_last.astype(full)).astype(low)
    dense_rows = 4 * local_width
    count = lax.axis_size("dp")
    dense = jnp.concatenate([weight_grad, out_weight_grad]).reshape(count, -1, model_width)
    dense, returned, down_one = tie(dense, returned, down_one)
    dense = jnp.sum(exchange(dense).astype(full), axis=0).astype(low)

    far_here = jnp.sum(far_grad, axis=1).reshape(2, heads_here)
    rel_grad = jnp.einsum("rb,hr->hb", lookup, near_grad, precision=highest)
    far_place = np.zeros((2, bucket_count), np.float32)
    far_place[0, bucket_count // 2 - 1] = 1.0
    far_place[1, bucket_count - 1] = 1.0
    rel_grad = rel_grad + jnp.sum(far_here[:, :, None] * far_place[:, None, :], axis=0)
    rel_place = (jnp.arange(groups, dtype=jnp.int32) == tensor_me).astype(full)
    rel_wide = rel_place[:, None, None] * rel_grad[None]
    flat = jnp.concatenate(
        [
            gain_one_grad.reshape(-1),
            gain_two_grad.reshape(-1),
            router_grad.reshape(-1),
            rel_wide.reshape(-1),
        ]
    )
    flat_rows = -(-flat.shape[0] // (16 * model_width)) * 16
    flat = flat + swap(flat, "tensor", 2)
    flat = flat + swap(flat, "tensor", 1)
    flat = jnp.pad(flat, (0, flat_rows * model_width - flat.shape[0]))
    payload = jnp.concatenate([dense, flat.reshape(flat_rows, model_width).astype(low)])
    across = swap(across_sent, "tensor", 2)
    rest = jnp.concatenate([up_sent[half:], down_two])
    payload, returned, up_one, across, rest = tie(payload, returned, up_one, across, rest)
    rest = swap(rest, "tensor", 2)
    payload = exchange(jnp.broadcast_to(payload[None], (count, *payload.shape)))
    dense, flat = payload[:, : dense_rows // count], payload[:, dense_rows // count :]
    dense = dense.reshape(dense_rows, model_width)

    normed_grad = rounded(own_part.astype(full) + beside_came + across.astype(full))
    inputs_f = hidden_in.astype(full)
    unused, scale_one = rms_forward(inputs_f, norm1_gain)
    input_part, unused = rms_backward(inputs_f, scale_one, norm1_gain, normed_grad)
    input_grad = middle_grad + input_part
    (layer_out,) = run_local(
        layer_kernel,
        "layer_output",
        [((row_count, model_width), low)],
        [],
        12 * 10**9,
        returned,
        position_col,
        expert_route.reshape(-1, 1),
        middle,
        normed_two,
        router_t,
    )
    layer_out, rest = tie(layer_out, rest)
    up_grad = up_near + jnp.concatenate([up_one, rest[:half]]).astype(full)
    down_grad = down_near + jnp.concatenate([down_one, rest[half:]]).astype(full)
    dense = dense.astype(full)
    flat = jnp.sum(flat.astype(full), axis=0).reshape(-1)
    gain_one_grad = flat[:model_width]
    gain_two_grad = flat[model_width : 2 * model_width]
    split = 2 * model_width + model_width * experts
    router_grad = flat[2 * model_width : split].reshape(experts, model_width).T
    rel_all = flat[split : split + groups * heads_here * bucket_count]
    rel_grad = pick(rel_all.reshape(groups, heads_here, bucket_count), tensor_me).T
    return (
        layer_out,
        input_grad,
        gain_one_grad,
        dense[:local_width].T,
        dense[local_width : 2 * local_width].T,
        dense[2 * local_width : 3 * local_width].T,
        dense[3 * local_width :],
        rel_grad,
        gain_two_grad,
        router_grad,
        up_grad[None],
        down_grad[None],
    )


def solution(mesh):
    return jax.shard_map(
        per_device,
        mesh=mesh,
        in_specs=(
            P(("dp", "tensor"), None),
            P("dp", None),
            P(("dp", "tensor")),
            P(("dp", "tensor")),
            P(),
            P(None, "tensor"),
            P(None, "tensor"),
            P(None, "tensor"),
            P("tensor", None),
            P(None, "tensor"),
            P(),
            P(),
            P("dp", None, "tensor"),
            P("dp", "tensor", None),
            P(("dp", "tensor"), None),
        ),
        out_specs=(
            P(("dp", "tensor"), None),
            P(("dp", "tensor"), None),
            P(),
            P(None, "tensor"),
            P(None, "tensor"),
            P(None, "tensor"),
            P("tensor", None),
            P(None, "tensor"),
            P(),
            P(),
            P("dp", None, "tensor"),
            P("dp", "tensor", None),
        ),
        check_vma=False,
    )
```
